32 devices in a mesh: dp: 8 (over z, core), expert: 4 (over y, x).
Axes of the slice: x: 2, y: 2, z: 4, core: 2. Of those that a mesh axis runs over, the one named last changes fastest.
Arguments:
- grad_out: bfloat16 [4096, 2048], P(('dp', 'expert')), may hold values from -6 to 6
- expert_ids: int32 [4096, 8], P(('dp', 'expert')), may hold values from 0 to 15, all different within a row; in each aligned block of 128 rows (0 to 127, 128 to 255, ...) at most 96 rows name the same one
- gate_weights: bfloat16 [4096, 8], P(('dp', 'expert')), may hold values from 0.019897461 to 0.5
- saved_hidden: bfloat16 [4, 3072, 768], P('expert', 'dp'), may hold values from -0.29882812 to 0.29882812
- down_weight: bfloat16 [4, 768, 2048], P('expert'), may hold values from -0.21875 to 0.21875
Outputs:
- hidden_grad: bfloat16 [4, 3072, 768], P('expert', 'dp')
- gate_grad: float32 [4096, 8], P(('dp', 'expert'))
- weight_grad: float32 [4, 2048, 768], P('expert', 'dp')
The draws below stay inside these ranges and needn't reach their ends.
Inputs may be any that keep to these rules, and one draw needn't show every extreme that they name: `expert_ids`: each row names 8 different experts; in the rows of one device (aligned blocks of 128 rows) no expert is named by more than 96 rows.
All inputs are finite; a program needn't handle non-finite values.
Results may differ from the reference program's by a relative error of at most 0.0029.
Values may be sent and summed in bfloat16 or wider, within the bound.
No kernel may reach another device: no remote copies, remote signals or barrier semaphores. Data moves between devices by JAX's collectives and lax.ppermute only.
A program may use at most 64 MiB of HBM per device.

```python
import math
import jax
import jax.numpy as jnp
import numpy as np
from jax import lax

DW = 2048
FFW = 768
TOP = 8
EXP_DEV = 4
TOK_DEV = 128
EXPERTS = 16
CAP = 96
TOKENS = 4096
N_DP = 8
N_EXPERT = 4


def raised(entries, own_key, source, target, parts, factor):
    def block_of(axis_at):
        return (jnp.arange(entries.shape[axis_at]) // (entries.shape[axis_at] // parts)).reshape((-1,) + (1,) * (entries.ndim - 1 - axis_at))

    first = jax.random.permutation(own_key, parts)[block_of(target)]
    far = (block_of(target) + parts // 2) % parts
    return jnp.where((block_of(source) == first) | (block_of(source) == far), factor * entries, entries)


def block_levels(stream_key, shape, cuts, low, largest):
    factor_of, own = 1.0, jax.random.fold_in(stream_key, 6)
    for axis_at, blocks in cuts:
        heights = jnp.exp(jax.random.uniform(jax.random.fold_in(own, axis_at), (blocks,), jnp.float32, low / len(cuts), largest / len(cuts)))
        factor_of = factor_of * jnp.repeat(heights, shape[axis_at] // blocks).reshape([-1 if axis == axis_at else 1 for axis in range(len(shape))])
    return factor_of


def deal_out(stream_key, own, number, rows, number_of, top, limit, lean):
    order = jax.random.permutation(stream_key, number_of)
    heavy_load, usual = load_shares(number_of, rows * top, limit, lean, True), load_shares(number_of, rows * top, limit, lean, False)
    places = jnp.arange(number_of)

    def named(tallies, rotation):
        used = int((tallies > 0).sum())
        fixed = max(1, used // 4)
        passed = fixed + (places - fixed + rotation * (used - fixed)) % max(1, number_of - fixed)
        return jnp.zeros((number_of,), jnp.int32).at[order[jnp.where(places < fixed, places, passed)]].set(jnp.asarray(tallies, jnp.int32))

    tallies = jnp.where(number % 4 == 0, named(heavy_load, number // 4), named(usual, number - number // 4 - 1))
    mixed = jax.random.permutation(jax.random.fold_in(own, 3), number_of)
    giver, sink = mixed[0:number_of // 2 * 2:2], mixed[1:number_of // 2 * 2:2]
    slack = jnp.minimum(tallies[giver] - 1, limit - tallies[sink]) // 2
    slack = jnp.where((giver == order[0]) | (sink == order[0]) | (tallies[sink] == 0), 0, jnp.maximum(slack, 0))
    passed = jax.random.randint(jax.random.fold_in(own, 4), (number_of // 2,), 0, 1 << 20) % (slack + 1)
    tallies = tallies.at[giver].add(-passed).at[sink].add(passed)
    items = jnp.searchsorted(jnp.cumsum(tallies), jnp.arange(rows * top), side="right").astype(jnp.int32)
    listing = items.reshape(top, rows).T
    listing = listing[jax.random.permutation(jax.random.fold_in(own, 1), rows)]
    rotation = jax.random.randint(jax.random.fold_in(own, 2), (rows, 1), 0, top)
    return jnp.take_along_axis(listing, (jnp.arange(top)[None, :] + rotation) % top, axis=1)


def load_shares(count, total, reach, slope, full):
    loads = [(1 << 20) // math.isqrt(grade ** slope) + 1 for grade in range(1, count + 1)]
    largest = reach if full else min(reach, max(-(-total // count), total * loads[0] // sum(loads)))
    least = 1 if total - largest >= count - 1 else 0
    counts, spare = [largest] + [least] * (count - 1), total - largest - least * (count - 1)
    while spare > 0:
        candidates = [i for i in range(1, count) if counts[i] < largest] or [i for i in range(1, count) if counts[i] < reach]
        pool, remaining = sum([loads[i] for i in candidates]), spare
        for i in candidates:
            extra = min(reach - counts[i], max(1, remaining * loads[i] // pool), spare)
            counts[i] = counts[i] + extra
            spare = spare - extra
    return np.array(counts)


def scatter_about(rng, extent, scale, most, pieces=(), kind=jnp.bfloat16):
    array = scale * jax.random.normal(rng, extent, jnp.float32)
    if pieces:
        array = array * block_levels(rng, extent, pieces, -0.22, 0.18)
    return jnp.clip(array, -most, most).astype(kind)


def heavy_noise(own_key, extent, width, bound, cuts, heavy, kind=jnp.bfloat16):
    values = width * jax.random.normal(own_key, extent, jnp.float32)
    if cuts:
        values = values * block_levels(own_key, extent, cuts, -0.22, 0.18)
    return jnp.clip(raised(values, jax.random.fold_in(own_key, 3), *heavy), -bound, bound).astype(kind)


def setup_inputs(seed: int = 0) -> dict:
    key_of = jax.random.split(jax.random.key(seed), 6)
    grad_out = scatter_about(key_of[0], (TOKENS, DW), 1.0, 6.0, ((0, 32),))
    expert_ids_keys = jax.random.split(jax.random.fold_in(key_of[1], 1), TOKENS // TOK_DEV)
    expert_ids_turns = jax.random.permutation(jax.random.fold_in(key_of[1], 3), TOKENS // TOK_DEV)
    expert_ids = jax.vmap(lambda own, number: deal_out(jax.random.fold_in(key_of[1], 2), own, number, TOK_DEV, EXPERTS, TOP, CAP, 2))(expert_ids_keys, expert_ids_turns).reshape((TOKENS, TOP))
    gate_weights = jnp.clip(jnp.exp(math.log(0.5) - 3.224016 * jax.random.uniform(key_of[2], (TOKENS, TOP), jnp.float32) ** block_levels(key_of[2], (TOKENS, TOP), ((0, 32),), -0.2, 0.2)), 0.019897461, 0.5).astype(jnp.bfloat16)
    saved_hidden = heavy_noise(key_of[3], (N_EXPERT, N_DP * N_EXPERT * CAP, FFW), 0.05, 0.29882812, ((0, 4), (1, 8)), (1, 2, 8, 2.0))
    down_weight = scatter_about(key_of[4], (N_EXPERT, FFW, DW), FFW ** -0.5, 0.21875, ((0, 4),))
    return dict(grad_out=grad_out, expert_ids=expert_ids, gate_weights=gate_weights, saved_hidden=saved_hidden, down_weight=down_weight)


def reference(grad_out, expert_ids, gate_weights, saved_hidden, down_weight):
    groups = N_DP
    peer_count = N_EXPERT
    pair_count = TOK_DEV * TOP
    routed = expert_ids.reshape(groups, peer_count, pair_count)
    flight = (routed % EXP_DEV) == 0
    target = routed // EXP_DEV
    onehot = ((target[..., None] == jnp.arange(peer_count, dtype=jnp.int32)) & flight[..., None]).astype(jnp.int32)
    slot_rank = jnp.cumsum(onehot, axis=2) - 1
    slot_index = jnp.sum(slot_rank * onehot, axis=3)
    slot_place = jnp.where(flight, target * CAP + slot_index, peer_count * CAP).astype(jnp.int32)
    token_index = jnp.broadcast_to(jnp.arange(pair_count, dtype=jnp.int32) // TOP, slot_place.shape)
    group_index = jnp.broadcast_to(jnp.arange(groups, dtype=jnp.int32)[:, None, None], slot_place.shape)
    source_index = jnp.broadcast_to(jnp.arange(peer_count, dtype=jnp.int32)[None, :, None], slot_place.shape)
    token_table = jnp.full((groups, peer_count, peer_count * CAP + 1), -1, jnp.int32)
    token_table = token_table.at[group_index, source_index, slot_place].set(token_index)[:, :, :-1]
    gates_flat = gate_weights.astype(jnp.float32).reshape(groups, peer_count, pair_count)
    gate_table = jnp.zeros((groups, peer_count, peer_count * CAP + 1), jnp.float32)
    gate_table = gate_table.at[group_index, source_index, slot_place].set(gates_flat)[:, :, :-1]
    grad_blocks = grad_out.reshape(groups, peer_count, TOK_DEV, DW)

    def one_expert(expert_slot):
        slot_token = lax.dynamic_slice_in_dim(token_table, expert_slot * CAP, CAP, 2)
        slot_gates = lax.dynamic_slice_in_dim(gate_table, expert_slot * CAP, CAP, 2).reshape(-1)
        filled = slot_token >= 0
        slot_rows = jnp.take_along_axis(grad_blocks, jnp.maximum(slot_token, 0)[..., None], axis=2)
        slot_rows = jnp.where(filled[..., None], slot_rows, jnp.zeros_like(slot_rows)).reshape(-1, DW)
        hidden = saved_hidden[expert_slot]
        weight = down_weight[expert_slot]
        update = jnp.dot(slot_rows, weight.T, preferred_element_type=jnp.float32)
        grad_hidden = (slot_gates[:, None] * update).astype(jnp.bfloat16)
        pair_grad = jnp.sum(hidden.astype(jnp.float32) * update, axis=1)
        scaled = (slot_gates[:, None] * hidden.astype(jnp.float32)).astype(jnp.bfloat16)
        grad_term = jnp.dot(slot_rows.T, scaled, preferred_element_type=jnp.float32)
        return grad_hidden, pair_grad.reshape(groups, peer_count, CAP), grad_term

    hidden_grad, pair_grad, weight_grad = lax.map(one_expert, jnp.arange(peer_count, dtype=jnp.int32))
    back_table = jnp.transpose(pair_grad, (1, 2, 0, 3)).reshape(groups, peer_count, peer_count * CAP)
    back_table = jnp.concatenate([back_table, jnp.zeros((groups, peer_count, 1), jnp.float32)], axis=2)
    gate_grad = jnp.take_along_axis(back_table, slot_place, axis=2).reshape(TOKENS, TOP)
    return hidden_grad, gate_grad, weight_grad
```

```python
import functools

import jax
import jax.numpy as jnp
from jax import lax
from jax.experimental import pallas as pl
from jax.experimental.pallas import tpu as pltpu
from jax.sharding import PartitionSpec as P

TOP = 8
EXP_DEV = 4
F32 = jnp.float32
BF16 = jnp.bfloat16
GATE_LANES = 128


def per_device_general(grad_out, expert_ids, gate_weights, saved_hidden, down_weight):
    peer_count = lax.axis_size("expert")
    tok_rows = grad_out.shape[0]
    capacity = saved_hidden.shape[1] // peer_count
    slot_total = peer_count * capacity
    flat_ids = expert_ids.reshape(-1)
    flight = flat_ids % EXP_DEV == 0
    target = flat_ids // EXP_DEV
    onehot = (
        (target[:, None] == jnp.arange(peer_count, dtype=jnp.int32)[None, :]) & flight[:, None]
    ).astype(jnp.int32)
    slot_rank = jnp.cumsum(onehot, axis=0) - 1
    slot_index = jnp.sum(slot_rank * onehot, axis=1)
    slot_place = jnp.where(flight, target * capacity + slot_index, slot_total)
    slot_match = slot_place[None, :] == jnp.arange(slot_total, dtype=jnp.int32)[:, None]
    gates_flat = gate_weights.astype(F32).reshape(-1)
    send_gates = jnp.sum(jnp.where(slot_match, gates_flat[None, :], 0.0), axis=1).astype(BF16)
    token_match = jnp.any(slot_match.reshape(slot_total, tok_rows, TOP), axis=2).astype(BF16)
    send_rows = jnp.dot(token_match, grad_out, preferred_element_type=F32).astype(BF16)
    exchange = functools.partial(
        lax.all_to_all, axis_name="expert", split_axis=0, concat_axis=0, tiled=True
    )
    rows_in = exchange(send_rows.reshape(peer_count, capacity, -1))
    gates_in = exchange(send_gates.reshape(peer_count, capacity))
    slot_rows = rows_in.reshape(slot_total, -1)
    slot_gates = gates_in.reshape(slot_total).astype(F32)
    hidden = saved_hidden[0]
    weight = down_weight[0]
    update = lax.dot_general(
        slot_rows, weight, (((1,), (1,)), ((), ())), preferred_element_type=F32
    )
    grad_hidden = (slot_gates[:, None] * update).astype(BF16)
    pair_grad = jnp.sum(hidden.astype(F32) * update, axis=1)
    returned = exchange(pair_grad.reshape(peer_count, capacity))
    gate_flat = jnp.sum(jnp.where(slot_match, returned.reshape(slot_total)[:, None], 0.0), axis=0)
    gate_grad = gate_flat.reshape(tok_rows, TOP)
    scaled = (slot_gates[:, None] * hidden.astype(F32)).astype(BF16)
    grad_term = lax.dot_general(
        slot_rows, scaled, (((0,), (0,)), ((), ())), preferred_element_type=F32
    )
    weight_shard = lax.psum_scatter(grad_term, "dp", scatter_dimension=0, tiled=True)
    return (grad_hidden[None], gate_grad, weight_shard[None])


def coordinates():
    group = lax.axis_index("dp")
    return group // 2, group % 2, lax.axis_index("expert")


def dot(a, b, dims):
    return lax.dot_general(a, b, (dims, ((), ())), preferred_element_type=F32)


def swap_kernel(block, ids_ref, gates_ref, grad_ref, send_ref, marks_ref):
    _, core, _ = coordinates()
    tokens = grad_ref.shape[0]
    ids = ids_ref[...]
    gates = gates_ref[...].astype(F32)
    experts = ids.shape[0] // 2
    marks_ref[...] = jnp.full(marks_ref.shape, -1.0, BF16)
    rows = []
    for j in range(experts):
        hit = ids == j * EXP_DEV
        value = jnp.sum(jnp.where(hit, gates, 0.0), axis=0, keepdims=True)
        live = jnp.sum(jnp.where(hit, 1.0, 0.0), axis=0, keepdims=True)
        rows.append(jnp.where(live > 0.0, value, -1.0))
    rows.append(jnp.full((marks_ref.shape[0] - experts, tokens), -1.0, F32))
    marks = jnp.concatenate(rows, axis=0).astype(BF16)
    marks_ref[...] = marks
    for i in range(send_ref.shape[1] // block):
        start = pl.multiple_of((2 * i + 1 - core) * block, block)
        send_ref[:tokens, i * block : (i + 1) * block] = grad_ref[:, pl.ds(start, block)]
    send_ref[tokens:, :] = jnp.zeros((16, send_ref.shape[1]), BF16)
    send_ref[tokens:, :tokens] = marks


def gather_kernel(block, capacity, grad_ref, marks_ref, other_ref, *outs):
    _first, matches_ref = outs[:-2], outs[-2]
    scratch = outs[-1]
    chip, core, peer = coordinates()
    tokens = grad_ref.shape[0]
    chunk = chip ^ 3
    before = (
        lax.broadcasted_iota(jnp.int32, (tokens, tokens), 0)
        < lax.broadcasted_iota(jnp.int32, (tokens, tokens), 1)
    ).astype(F32).astype(BF16)
    slot = lax.broadcasted_iota(jnp.int32, (capacity, tokens), 0).astype(F32)
    own = grad_ref[:, pl.ds(pl.multiple_of((2 * chunk + core) * block, block), block)]
    other = other_ref[:tokens, pl.ds(pl.multiple_of(chunk * block, block), block)]
    for g in range(2):
        marks = (marks_ref[...] if g == 0 else other_ref[tokens:, :tokens]).astype(F32)
        live = jnp.where(marks >= 0.0, 1.0, 0.0)
        rank = dot(live.astype(BF16), before, ((1,), (0,)))
        scratch[2 * g] = marks
        scratch[2 * g + 1] = jnp.where(marks >= 0.0, rank, -1.0)
        rows = own if g == 0 else other
        for r in range(4):
            e = peer ^ r
            gate = scratch[2 * g, pl.ds(e, 1), :]
            place = scratch[2 * g + 1, pl.ds(e, 1), :]
            match = slot == place
            matchb = jnp.where(match, 1.0, 0.0).astype(BF16)
            matches_ref[g, r] = matchb
            column = jnp.sum(jnp.where(match, gate, 0.0), axis=1, keepdims=True)
            at = slice(g * capacity, (g + 1) * capacity)
            _first[r][at, :block] = dot(matchb, rows, ((1,), (0,))).astype(BF16)
            _first[r][at, block:] = jnp.broadcast_to(column, (capacity, GATE_LANES)).astype(BF16)


def rest_kernel(block, capacity, grad_ref, other_ref, matches_ref, *outs):
    chip, core, _ = coordinates()
    tokens = grad_ref.shape[0]
    for k in range(1, 4):
        chunk = chip ^ (3 - k)
        own = grad_ref[:, pl.ds(pl.multiple_of((2 * chunk + core) * block, block), block)]
        other = other_ref[:tokens, pl.ds(pl.multiple_of(chunk * block, block), block)]
        to = slice(0, block) if k < 3 else slice(block, 2 * block)
        for g in range(2):
            for r in range(4):
                out = outs[r if k == 1 else 4 + r]
                out[g * capacity : (g + 1) * capacity, to] = dot(
                    matches_ref[g, r], own if g == 0 else other, ((1,), (0,))
                ).astype(BF16)


def first_kernel(block, capacity, p0, p1, p2, p3, hidden_ref, other_ref, part_ref, scaled_ref, rows_ref):
    _, _, peer = coordinates()
    for r, piece in enumerate((p0, p1, p2, p3)):
        source = pl.ds(pl.multiple_of((peer ^ r) * capacity, 32), capacity)
        for g, hidden in enumerate((hidden_ref, other_ref)):
            at = slice((2 * r + g) * capacity, (2 * r + g + 1) * capacity)
            gate = piece[g * capacity : (g + 1) * capacity, block : block + 1].astype(F32)
            scaled_ref[at, :] = (gate * hidden[source, :].astype(F32)).astype(BF16)
            rows_ref[at, :] = piece[g * capacity : (g + 1) * capacity, :block]
    part_ref[...] = dot(rows_ref[...], scaled_ref[...], ((0,), (0,))).astype(part_ref.dtype)


def part_kernel(p0, p1, p2, p3, scaled_ref, *outs):
    *parts, rows_ref = outs
    size = p0.shape[0]
    for r, piece in enumerate((p0, p1, p2, p3)):
        rows_ref[r * size : (r + 1) * size, :] = piece[...]
    block = parts[0].shape[0]
    for i, part in enumerate(parts):
        part[...] = dot(
            rows_ref[:, i * block : (i + 1) * block], scaled_ref[...], ((0,), (0,))
        ).astype(part.dtype)


def update_kernel(block, capacity, rows0, rows1, rows23, weight_ref, own_ref, other_ref):
    chip, core, _ = coordinates()
    total = None
    for k in range(4):
        start = pl.multiple_of((2 * (chip ^ (3 - k)) + core) * block, block)
        rows = (rows0, rows1, rows23, rows23)[k]
        at = slice(block, 2 * block) if k == 3 else slice(0, block)
        term = dot(rows[:, at], weight_ref[:, pl.ds(start, block)], ((1,), (1,)))
        total = term if total is None else total + term
    for r in range(4):
        to = slice(r * capacity, (r + 1) * capacity)
        own_ref[to, :] = total[2 * r * capacity : (2 * r + 1) * capacity, :]
        other_ref[to, :] = total[(2 * r + 1) * capacity : (2 * r + 2) * capacity, :]


def hidden_kernel(block, capacity, own_ref, come_ref, p0, p1, p2, p3, hidden_ref, out_ref, *pairs):
    _, _, peer = coordinates()
    for r, piece in enumerate((p0, p1, p2, p3)):
        at = slice(r * capacity, (r + 1) * capacity)
        source = pl.ds(pl.multiple_of((peer ^ r) * capacity, 32), capacity)
        update = own_ref[at, :] + come_ref[at, :]
        gate = piece[:capacity, block : block + 1].astype(F32)
        out_ref[source, :] = (gate * update).astype(BF16)
        pair = jnp.sum(hidden_ref[source, :].astype(F32) * update, axis=1, keepdims=True)
        pairs[r][...] = jnp.broadcast_to(pair, (capacity, 128))


def gate_kernel(ids_ref, matches_ref, b0, b1, b2, b3, out_ref):
    _, _, peer = coordinates()
    ids = ids_ref[...]
    total = jnp.zeros(ids.shape, F32)
    for r, back in enumerate((b0, b1, b2, b3)):
        at_token = jnp.sum(
            jnp.where(matches_ref[0, r].astype(F32) > 0.0, back[...], 0.0), axis=0, keepdims=True
        )
        total = jnp.where(ids == (peer ^ r) * EXP_DEV, at_token, total)
    out_ref[...] = total


def call(kernel, outs, flops=0, scratch=()):
    size = lambda s: s.size * s.dtype.itemsize
    multiple = isinstance(outs, (list, tuple))
    every = outs if multiple else [outs]

    def run(*args):
        moved = sum(size(a) for a in args) + sum(size(o) for o in every)
        return pl.pallas_call(
            kernel,
            out_shape=outs,
            scratch_shapes=list(scratch),
            compiler_params=pltpu.CompilerParams(vmem_limit_bytes=40 * 2**20),
            cost_estimate=pl.CostEstimate(flops=flops, bytes_accessed=moved, transcendentals=0),
        )(*args)

    return run


def arr(shape, dtype):
    return jax.ShapeDtypeStruct(shape, dtype)


def over(axis, size, mask):
    pairs = [(i, i ^ mask) for i in range(size)]
    return lambda x: lax.ppermute(x, axis, pairs)


def per_device(grad_out, expert_ids, gate_weights, saved_hidden, down_weight):
    groups, peers = lax.axis_size("dp"), lax.axis_size("expert")
    tokens, features = grad_out.shape
    hidden, weight = saved_hidden[0], down_weight[0]
    slots, units = hidden.shape
    capacity = slots // peers
    block = features // groups
    half = features // 2
    core_swap, near, far = (over("dp", groups, m) for m in (1, 2, 4))
    to_peer = [lambda x: x] + [over("expert", peers, r) for r in range(1, peers)]
    ids_t, gates_t = expert_ids.T, gate_weights.T

    send, marks = call(
        functools.partial(swap_kernel, block),
        [arr((tokens + 16, half), BF16), arr((16, tokens), BF16)],
    )(ids_t, gates_t, grad_out)
    other = core_swap(send)
    other_hidden = core_swap(hidden)
    *first, matches = call(
        functools.partial(gather_kernel, block, capacity),
        [arr((2 * capacity, block + GATE_LANES), BF16)] * peers
        + [arr((2, peers, capacity, tokens), BF16)],
        flops=4 * peers * capacity * tokens * block,
        scratch=[pltpu.VMEM((4, 16, tokens), F32)],
    )(grad_out, marks, other)
    first = [to_peer[r](first[r]) for r in range(peers)]
    rest = call(
        functools.partial(rest_kernel, block, capacity),
        [arr((2 * capacity, block), BF16)] * peers + [arr((2 * capacity, 2 * block), BF16)] * peers,
        flops=12 * peers * capacity * tokens * block,
    )(grad_out, other, matches)
    second = [to_peer[r](rest[r]) for r in range(peers)]
    third = [to_peer[r](rest[peers + r]) for r in range(peers)]

    part_flops = 2 * block * 2 * slots * units
    part0, scaled, rows0 = call(
        functools.partial(first_kernel, block, capacity),
        [arr((block, units), BF16), arr((2 * slots, units), BF16), arr((2 * slots, block), BF16)],
        flops=part_flops,
    )(*first, hidden, other_hidden)
    come0 = near(part0)
    part1, rows1 = call(
        part_kernel,
        [arr((block, units), F32), arr((2 * slots, block), BF16)],
        flops=part_flops,
    )(*second, scaled)
    come1 = far((part1 + come0.astype(F32)).astype(BF16))
    part2, part3, rows23 = call(
        part_kernel,
        [arr((block, units), BF16), arr((block, units), F32), arr((2 * slots, 2 * block), BF16)],
        flops=2 * part_flops,
    )(*third, scaled)
    come2 = near(part2)
    mine, theirs = call(
        functools.partial(update_kernel, block, capacity),
        [arr((slots, units), F32)] * 2,
        flops=4 * part_flops,
    )(rows0, rows1, rows23, weight)
    update = core_swap(theirs)
    grad_hidden, *pairs = call(
        functools.partial(hidden_kernel, block, capacity),
        [arr((slots, units), BF16)] + [arr((capacity, 128), F32)] * peers,
    )(mine, update, *first, hidden)
    back = [to_peer[r](pairs[r]) for r in range(peers)]
    gate_grad = call(gate_kernel, arr((TOP, tokens), F32))(ids_t, matches, *back).T
    weight_grad = part3 + come2.astype(F32) + come1.astype(F32)
    return grad_hidden[None], gate_grad, weight_grad[None]


def solution(mesh):
    placed = (
        P(("dp", "expert"), None),
        P(("dp", "expert"), None),
        P(("dp", "expert"), None),
        P("expert", "dp", None),
        P("expert", None, None),
    )
    small = mesh.shape["dp"] == 8 and mesh.shape["expert"] == 4
    return jax.shard_map(
        per_device if small else per_device_general,
        mesh=mesh,
        in_specs=placed,
        out_specs=(P("expert", "dp", None), P(("dp", "expert"), None), P("expert", "dp", None)),
        check_vma=False,
    )
```

```python
import functools

import jax
import jax.numpy as jnp
from jax import lax
from jax.experimental import pallas as pl
from jax.experimental.pallas import tpu as pltpu
from jax.sharding import PartitionSpec as P

TOP = 8
EXP_DEV = 4
F32 = jnp.float32
BF16 = jnp.bfloat16
GATE_LANES = 128


def per_device_general(grad_out, expert_ids, gate_weights, saved_hidden, down_weight):
    peer_count = lax.axis_size("expert")
    tok_rows = grad_out.shape[0]
    capacity = saved_hidden.shape[1] // peer_count
    slot_total = peer_count * capacity
    flat_ids = expert_ids.reshape(-1)
    flight = flat_ids % EXP_DEV == 0
    target = flat_ids // EXP_DEV
    onehot = (
        (target[:, None] == jnp.arange(peer_count, dtype=jnp.int32)[None, :]) & flight[:, None]
    ).astype(jnp.int32)
    slot_rank = jnp.cumsum(onehot, axis=0) - 1
    slot_index = jnp.sum(slot_rank * onehot, axis=1)
    slot_place = jnp.where(flight, target * capacity + slot_index, slot_total)
    slot_match = slot_place[None, :] == jnp.arange(slot_total, dtype=jnp.int32)[:, None]
    gates_flat = gate_weights.astype(F32).reshape(-1)
    send_gates = jnp.sum(jnp.where(slot_match, gates_flat[None, :], 0.0), axis=1).astype(BF16)
    token_match = jnp.any(slot_match.reshape(slot_total, tok_rows, TOP), axis=2).astype(BF16)
    send_rows = jnp.dot(token_match, grad_out, preferred_element_type=F32).astype(BF16)
    exchange = functools.partial(
        lax.all_to_all, axis_name="expert", split_axis=0, concat_axis=0, tiled=True
    )
    rows_in = exchange(send_rows.reshape(peer_count, capacity, -1))
    gates_in = exchange(send_gates.reshape(peer_count, capacity))
    slot_rows = rows_in.reshape(slot_total, -1)
    slot_gates = gates_in.reshape(slot_total).astype(F32)
    hidden = saved_hidden[0]
    weight = down_weight[0]
    update = lax.dot_general(
        slot_rows, weight, (((1,), (1,)), ((), ())), preferred_element_type=F32
    )
    grad_hidden = (slot_gates[:, None] * update).astype(BF16)
    pair_grad = jnp.sum(hidden.astype(F32) * update, axis=1)
    returned = exchange(pair_grad.reshape(peer_count, capacity))
    gate_flat = jnp.sum(jnp.where(slot_match, returned.reshape(slot_total)[:, None], 0.0), axis=0)
    gate_grad = gate_flat.reshape(tok_rows, TOP)
    scaled = (slot_gates[:, None] * hidden.astype(F32)).astype(BF16)
    grad_term = lax.dot_general(
        slot_rows, scaled, (((0,), (0,)), ((), ())), preferred_element_type=F32
    )
    weight_shard = lax.psum_scatter(grad_term, "dp", scatter_dimension=0, tiled=True)
    return (grad_hidden[None], gate_grad, weight_shard[None])


def coordinates():
    group = lax.axis_index("dp")
    return group // 2, group % 2, lax.axis_index("expert")


def dot(a, b, dims):
    return lax.dot_general(a, b, (dims, ((), ())), preferred_element_type=F32)


def swap_kernel(block, ids_hbm, gates_hbm, grad_hbm, send_ref, own_ref, marks_ref, ids_ref, gates_ref, sems):
    _, core, _ = coordinates()
    tokens = grad_hbm.shape[0]
    count = own_ref.shape[1] // block
    copies = [
        pltpu.make_async_copy(ids_hbm, ids_ref, sems.at[0]),
        pltpu.make_async_copy(gates_hbm, gates_ref, sems.at[1]),
    ]
    for i in range(count):
        at = slice(i * block, (i + 1) * block)
        for n, (side, ref) in enumerate(((1 - core, send_ref), (core, own_ref))):
            start = pl.multiple_of((2 * i + side) * block, block)
            copies.append(
                pltpu.make_async_copy(
                    grad_hbm.at[:, pl.ds(start, block)],
                    ref.at[pl.ds(0, tokens), at],
                    sems.at[2 + 2 * i + n],
                )
            )
    for copy in copies:
        copy.start()
    send_ref[tokens:, :] = jnp.zeros((16, send_ref.shape[1]), BF16)
    copies[0].wait()
    copies[1].wait()
    ids = ids_ref[...]
    gates = gates_ref[...].astype(F32)
    experts = ids.shape[0] // 2
    rows = []
    for j in range(experts):
        hit = ids == j * EXP_DEV
        value = jnp.sum(jnp.where(hit, gates, 0.0), axis=0, keepdims=True)
        live = jnp.sum(jnp.where(hit, 1.0, 0.0), axis=0, keepdims=True)
        rows.append(jnp.where(live > 0.0, value, -1.0))
    rows.append(jnp.full((marks_ref.shape[0] - experts, tokens), -1.0, F32))
    marks = jnp.concatenate(rows, axis=0).astype(BF16)
    marks_ref[...] = marks
    send_ref[tokens:, :tokens] = marks
    for copy in copies[2:]:
        copy.wait()


def gather_kernel(block, capacity, own_ref, marks_ref, other_ref, hidden_hbm, *outs):
    first, (matches_ref, hidden_ref, scratch, sem) = outs[:-4], outs[-4:]
    copy = pltpu.make_async_copy(hidden_hbm, hidden_ref, sem)
    copy.start()
    chip, _, peer = coordinates()
    tokens = own_ref.shape[0]
    before = (
        lax.broadcasted_iota(jnp.int32, (tokens, tokens), 0)
        < lax.broadcasted_iota(jnp.int32, (tokens, tokens), 1)
    ).astype(F32).astype(BF16)
    slot = lax.broadcasted_iota(jnp.int32, (capacity, tokens), 0).astype(F32)
    columns = pl.ds(pl.multiple_of((chip ^ 3) * block, block), block)
    gate_rows = [[], [], [], []]
    for g in range(2):
        marks = (marks_ref[...] if g == 0 else other_ref[tokens:, :tokens]).astype(F32)
        live = jnp.where(marks >= 0.0, 1.0, 0.0)
        rank = dot(live.astype(BF16), before, ((1,), (0,)))
        scratch[2 * g] = marks
        scratch[2 * g + 1] = jnp.where(marks >= 0.0, rank, -1.0)
        rows = (own_ref if g == 0 else other_ref)[:tokens, columns]
        for r in range(4):
            e = peer ^ r
            gate = scratch[2 * g, pl.ds(e, 1), :]
            place = scratch[2 * g + 1, pl.ds(e, 1), :]
            match = jnp.where(slot == place, 1.0, 0.0).astype(BF16)
            matches_ref[g, r] = match
            gate_rows[r].append(
                dot(jnp.broadcast_to(gate, (16, tokens)).astype(BF16), match, ((1,), (1,)))
            )
            first[r][g * capacity : (g + 1) * capacity, :] = dot(
                match, rows, ((1,), (0,))
            ).astype(BF16)
    row = lax.broadcasted_iota(jnp.int32, (16, capacity), 0)
    for r in range(4):
        both = jnp.where(row == 0, gate_rows[r][0], jnp.where(row == 1, gate_rows[r][1], 0.0))
        first[r][2 * capacity :, :] = jnp.zeros((16, first[r].shape[1]), BF16)
        first[r][2 * capacity :, :capacity] = both.astype(BF16)
    copy.wait()


def gate_column(piece, g, capacity):
    row = piece[2 * capacity :, :128].astype(F32)[g : g + 1, :]
    here = lax.broadcasted_iota(jnp.int32, (capacity, 128), 0) == lax.broadcasted_iota(
        jnp.int32, (capacity, 128), 1
    )
    return jnp.sum(jnp.where(here, row, 0.0), axis=1, keepdims=True)


def rest_kernel(block, capacity, chunks, own_ref, other_ref, matches_ref, *outs):
    chip, _, _ = coordinates()
    tokens = own_ref.shape[0]
    for i, k in enumerate(chunks):
        columns = pl.ds(pl.multiple_of((chip ^ (3 - k)) * block, block), block)
        to = slice(i * block, (i + 1) * block)
        for g in range(2):
            rows = (own_ref if g == 0 else other_ref)[:tokens, columns]
            for r in range(4):
                outs[r - 4][g * capacity : (g + 1) * capacity, to] = dot(
                    matches_ref[g, r], rows, ((1,), (0,))
                ).astype(BF16)


def split_rows(pieces, at_columns, capacity, all_ref, own_ref, cross_ref):
    slots = 4 * capacity
    for r, piece in enumerate(pieces):
        at = slice(r * capacity, (r + 1) * capacity)
        mine = piece[:capacity, at_columns]
        cross = piece[capacity : 2 * capacity, at_columns]
        own_ref[at, :] = mine
        cross_ref[at, :] = cross
        all_ref[at, :] = mine
        all_ref[slots + r * capacity : slots + (r + 1) * capacity, :] = cross


def first_kernel(
    capacity, p0, p1, p2, p3, hidden_ref, other_ref, low_ref, high_ref, scaled_ref, own_ref, cross_ref, all_ref
):
    _, _, peer = coordinates()
    pieces = (p0, p1, p2, p3)
    for r, piece in enumerate(pieces):
        source = pl.ds(pl.multiple_of((peer ^ r) * capacity, 32), capacity)
        for g, hidden in enumerate((hidden_ref, other_ref)):
            at = slice((4 * g + r) * capacity, (4 * g + r + 1) * capacity)
            gate = gate_column(piece, g, capacity)
            scaled_ref[at, :] = (gate * hidden[source, :].astype(F32)).astype(BF16)
    split_rows(pieces, slice(None), capacity, all_ref, own_ref, cross_ref)
    part = dot(all_ref[...], scaled_ref[...], ((0,), (0,))).astype(BF16)
    half = low_ref.shape[0]
    low_ref[...] = part[:half, :]
    high_ref[...] = part[half:, :]


def second_kernel(capacity, p0, p1, p2, p3, scaled_ref, low_ref, high_ref, sum_ref, own_ref, cross_ref, all_ref):
    block = own_ref.shape[1]
    split_rows((p0, p1, p2, p3), slice(0, block), capacity, all_ref, own_ref, cross_ref)
    part = dot(all_ref[...], scaled_ref[...], ((0,), (0,)))
    half = low_ref.shape[0]
    sum_ref[:half, :] = (part[:half, :] + low_ref[...].astype(F32)).astype(BF16)
    sum_ref[half:, :] = (part[half:, :] + high_ref[...].astype(F32)).astype(BF16)


def last_kernel(capacity, p0, p1, p2, p3, scaled_ref, _, part2_ref, part3_ref, own2, cross2, own3, cross3, all_ref):
    for i, (part, own, cross) in enumerate(((part2_ref, own2, cross2), (part3_ref, own3, cross3))):
        block = own.shape[1]
        at = slice((i + 1) * block, (i + 2) * block)
        split_rows((p0, p1, p2, p3), at, capacity, all_ref.at[i], own, cross)
        part[...] = dot(all_ref[i], scaled_ref[...], ((0,), (0,))).astype(part.dtype)


def update_kernel(capacity, *refs):
    rows, (p0, p1, p2, p3, hidden_ref, weight_ref, out_ref, *pairs) = refs[:8], refs[8:]
    chip, core, peer = coordinates()
    block = rows[0].shape[1]
    update = None
    for k in range(4):
        for i, side in enumerate((core, 1 - core)):
            start = pl.multiple_of((2 * (chip ^ (3 - k)) + side) * block, block)
            term = dot(rows[2 * k + i][...], weight_ref[:, pl.ds(start, block)], ((1,), (1,)))
            update = term if update is None else update + term
    for r, piece in enumerate((p0, p1, p2, p3)):
        source = pl.ds(pl.multiple_of((peer ^ r) * capacity, 32), capacity)
        here = update[r * capacity : (r + 1) * capacity, :]
        out_ref[source, :] = (gate_column(piece, 0, capacity) * here).astype(BF16)
        pair = jnp.sum(hidden_ref[source, :].astype(F32) * here, axis=1, keepdims=True)
        pairs[r][...] = jnp.broadcast_to(pair, (capacity, 128))


def gate_kernel(ids_ref, matches_ref, b0, b1, b2, b3, out_ref):
    _, _, peer = coordinates()
    ids = ids_ref[...]
    total = jnp.zeros(ids.shape, F32)
    for r, back in enumerate((b0, b1, b2, b3)):
        at_token = jnp.sum(
            jnp.where(matches_ref[0, r].astype(F32) > 0.0, back[...], 0.0), axis=0, keepdims=True
        )
        total = jnp.where(ids == (peer ^ r) * EXP_DEV, at_token, total)
    out_ref[...] = total


HBM = pl.BlockSpec(memory_space=pltpu.HBM)
ANY = pl.BlockSpec(memory_space=pl.ANY)
VMEM = pl.BlockSpec(memory_space=pltpu.VMEM)


def call(kernel, outs, specs=None, scratch=(), vmem=40 * 2**20):
    def run(*args):
        return pl.pallas_call(
            kernel,
            out_shape=outs,
            in_specs=specs or [VMEM] * len(args),
            out_specs=jax.tree.map(lambda _: VMEM, outs),
            scratch_shapes=list(scratch),
            compiler_params=pltpu.CompilerParams(vmem_limit_bytes=vmem),
            cost_estimate=pl.CostEstimate(flops=0, bytes_accessed=0, transcendentals=0),
        )(*args)

    return run


def arr(shape, dtype):
    return jax.ShapeDtypeStruct(shape, dtype)


def over(axis, size, mask):
    pairs = [(i, i ^ mask) for i in range(size)]
    return lambda x: lax.ppermute(x, axis, pairs)


def per_device(grad_out, expert_ids, gate_weights, saved_hidden, down_weight):
    groups, peers = lax.axis_size("dp"), lax.axis_size("expert")
    tokens, features = grad_out.shape
    hidden, weight = saved_hidden[0], down_weight[0]
    slots, units = hidden.shape
    capacity = slots // peers
    block = features // groups
    half = features // 2
    core_swap, near, far = (over("dp", groups, m) for m in (1, 2, 4))
    to_peer = [lambda x: x] + [over("expert", peers, r) for r in range(1, peers)]
    ids_t, gates_t = expert_ids.T, gate_weights.T

    send, own, marks = call(
        functools.partial(swap_kernel, block),
        [arr((tokens + 16, half), BF16), arr((tokens, half), BF16), arr((16, tokens), BF16)],
        specs=[HBM] * 3,
        scratch=[
            pltpu.VMEM((TOP, tokens), jnp.int32),
            pltpu.VMEM((TOP, tokens), BF16),
            pltpu.SemaphoreType.DMA((2 + groups,)),
        ],
    )(ids_t, gates_t, grad_out)
    other = core_swap(send)
    *first, matches, hidden = call(
        functools.partial(gather_kernel, block, capacity),
        [arr((2 * capacity + 16, block), BF16)] * peers
        + [arr((2, peers, capacity, tokens), BF16), arr((slots, units), BF16)],
        specs=[VMEM] * 3 + [HBM],
        scratch=[pltpu.VMEM((4, 16, tokens), F32), pltpu.SemaphoreType.DMA],
    )(own, marks, other, hidden)
    first = [to_peer[r](first[r]) for r in range(peers)]
    other_hidden = core_swap(hidden)

    def later(chunks, *after):
        pieces = call(
            functools.partial(rest_kernel, block, capacity, chunks),
            [arr((2 * capacity, len(chunks) * block), BF16)] * peers,
            specs=[VMEM] * 3 + [ANY] * len(after),
        )(own, other, matches, *after)
        return [to_peer[r](pieces[r]) for r in range(peers)]

    rest = later((1, 2, 3), matches)
    stack = (2 * slots, block)
    mine = arr((slots, block), BF16)
    low, high, scaled, own0, cross0 = call(
        functools.partial(first_kernel, capacity),
        [arr((block // 2, units), BF16)] * 2 + [arr((2 * slots, units), BF16), mine, mine],
        scratch=[pltpu.VMEM(stack, BF16)],
    )(*first, hidden, other_hidden)
    low, high = near(low), near(high)
    summed, own1, cross1 = call(
        functools.partial(second_kernel, capacity),
        [arr((block, units), BF16), mine, mine],
        scratch=[pltpu.VMEM(stack, BF16)],
    )(*rest, scaled, low, high)
    come1 = far(summed)
    part2, part3, own2, cross2, own3, cross3 = call(
        functools.partial(last_kernel, capacity),
        [arr((block, units), BF16), arr((block, units), F32), mine, mine, mine, mine],
        specs=[VMEM] * 5 + [ANY],
        scratch=[pltpu.VMEM((2,) + stack, BF16)],
    )(*rest, scaled, summed)
    come2 = near(part2)
    rows = []
    for own_k, cross_k in ((own0, cross0), (own1, cross1), (own2, cross2), (own3, cross3)):
        rows += [own_k, core_swap(cross_k)]
    grad_hidden, *pairs = call(
        functools.partial(update_kernel, capacity),
        [arr((slots, units), BF16)] + [arr((capacity, 128), F32)] * peers,
    )(*rows, *first, hidden, weight)
    back = [to_peer[r](pairs[r]) for r in range(peers)]
    gate_grad = call(gate_kernel, arr((TOP, tokens), F32))(ids_t, matches, *back).T
    weight_grad = part3 + come2.astype(F32) + come1.astype(F32)
    return grad_hidden[None], gate_grad, weight_grad[None]


def solution(mesh):
    placed = (
        P(("dp", "expert"), None),
        P(("dp", "expert"), None),
        P(("dp", "expert"), None),
        P("expert", "dp", None),
        P("expert", None, None),
    )
    small = mesh.shape["dp"] == 8 and mesh.shape["expert"] == 4
    return jax.shard_map(
        per_device if small else per_device_general,
        mesh=mesh,
        in_specs=placed,
        out_specs=(P("expert", "dp", None), P(("dp", "expert"), None), P("expert", "dp", None)),
        check_vma=False,
    )
```

```python
import functools

import jax
import jax.numpy as jnp
from jax import lax
from jax.experimental import pallas as pl
from jax.experimental.pallas import tpu as pltpu
from jax.sharding import PartitionSpec as P

TOP = 8
EXP_DEV = 4
F32 = jnp.float32
BF16 = jnp.bfloat16
GATE_LANES = 128


def per_device_general(grad_out, expert_ids, gate_weights, saved_hidden, down_weight):
    peer_count = lax.axis_size("expert")
    tok_rows = grad_out.shape[0]
    capacity = saved_hidden.shape[1] // peer_count
    slot_total = peer_count * capacity
    flat_ids = expert_ids.reshape(-1)
    flight = flat_ids % EXP_DEV == 0
    target = flat_ids // EXP_DEV
    onehot = (
        (target[:, None] == jnp.arange(peer_count, dtype=jnp.int32)[None, :]) & flight[:, None]
    ).astype(jnp.int32)
    slot_rank = jnp.cumsum(onehot, axis=0) - 1
    slot_index = jnp.sum(slot_rank * onehot, axis=1)
    slot_place = jnp.where(flight, target * capacity + slot_index, slot_total)
    slot_match = slot_place[None, :] == jnp.arange(slot_total, dtype=jnp.int32)[:, None]
    gates_flat = gate_weights.astype(F32).reshape(-1)
    send_gates = jnp.sum(jnp.where(slot_match, gates_flat[None, :], 0.0), axis=1).astype(BF16)
    token_match = jnp.any(slot_match.reshape(slot_total, tok_rows, TOP), axis=2).astype(BF16)
    send_rows = jnp.dot(token_match, grad_out, preferred_element_type=F32).astype(BF16)
    exchange = functools.partial(
        lax.all_to_all, axis_name="expert", split_axis=0, concat_axis=0, tiled=True
    )
    rows_in = exchange(send_rows.reshape(peer_count, capacity, -1))
    gates_in = exchange(send_gates.reshape(peer_count, capacity))
    slot_rows = rows_in.reshape(slot_total, -1)
    slot_gates = gates_in.reshape(slot_total).astype(F32)
    hidden = saved_hidden[0]
    weight = down_weight[0]
    update = lax.dot_general(
        slot_rows, weight, (((1,), (1,)), ((), ())), preferred_element_type=F32
    )
    grad_hidden = (slot_gates[:, None] * update).astype(BF16)
    pair_grad = jnp.sum(hidden.astype(F32) * update, axis=1)
    returned = exchange(pair_grad.reshape(peer_count, capacity))
    gate_flat = jnp.sum(jnp.where(slot_match, returned.reshape(slot_total)[:, None], 0.0), axis=0)
    gate_grad = gate_flat.reshape(tok_rows, TOP)
    scaled = (slot_gates[:, None] * hidden.astype(F32)).astype(BF16)
    grad_term = lax.dot_general(
        slot_rows, scaled, (((0,), (0,)), ((), ())), preferred_element_type=F32
    )
    weight_shard = lax.psum_scatter(grad_term, "dp", scatter_dimension=0, tiled=True)
    return (grad_hidden[None], gate_grad, weight_shard[None])


def coordinates():
    group = lax.axis_index("dp")
    return group // 2, group % 2, lax.axis_index("expert")


def dot(a, b, dims):
    return lax.dot_general(a, b, (dims, ((), ())), preferred_element_type=F32)


def swap_kernel(block, marks_in, grad_ref, send_ref, own_ref, marks_ref):
    _, core, _ = coordinates()
    tokens = grad_ref.shape[0]
    for i in range(own_ref.shape[1] // block):
        at = slice(i * block, (i + 1) * block)
        for side, ref in ((1 - core, send_ref), (core, own_ref)):
            start = pl.multiple_of((2 * i + side) * block, block)
            ref[:tokens, at] = grad_ref[:, pl.ds(start, block)]
    marks = jnp.concatenate([marks_in[...], jnp.full((12, tokens), -1.0, F32)], axis=0)
    marks_ref[...] = marks.astype(BF16)
    send_ref[tokens:, :] = jnp.zeros((16, send_ref.shape[1]), BF16)
    send_ref[tokens:, :tokens] = marks.astype(BF16)


def gather_kernel(block, capacity, own_ref, marks_ref, other_ref, *outs):
    first, (matches_ref, scratch) = outs[:-2], outs[-2:]
    chip, _, peer = coordinates()
    tokens = own_ref.shape[0]
    before = (
        lax.broadcasted_iota(jnp.int32, (tokens, tokens), 0)
        < lax.broadcasted_iota(jnp.int32, (tokens, tokens), 1)
    ).astype(F32).astype(BF16)
    slot = lax.broadcasted_iota(jnp.int32, (capacity, tokens), 0).astype(F32)
    columns = pl.ds(pl.multiple_of((chip ^ 3) * block, block), block)
    gate_rows = [[], [], [], []]
    for g in range(2):
        marks = (marks_ref[...] if g == 0 else other_ref[tokens:, :tokens]).astype(F32)
        live = jnp.where(marks >= 0.0, 1.0, 0.0)
        rank = dot(live.astype(BF16), before, ((1,), (0,)))
        scratch[2 * g] = marks
        scratch[2 * g + 1] = jnp.where(marks >= 0.0, rank, -1.0)
        rows = (own_ref if g == 0 else other_ref)[:tokens, columns]
        for r in range(4):
            e = peer ^ r
            gate = scratch[2 * g, pl.ds(e, 1), :]
            place = scratch[2 * g + 1, pl.ds(e, 1), :]
            match = jnp.where(slot == place, 1.0, 0.0).astype(BF16)
            matches_ref[g, r] = match
            gate_rows[r].append(
                dot(jnp.broadcast_to(gate, (16, tokens)).astype(BF16), match, ((1,), (1,)))
            )
            first[r][g * capacity : (g + 1) * capacity, :] = dot(
                match, rows, ((1,), (0,))
            ).astype(BF16)
    row = lax.broadcasted_iota(jnp.int32, (16, capacity), 0)
    for r in range(4):
        both = jnp.where(row == 0, gate_rows[r][0], jnp.where(row == 1, gate_rows[r][1], 0.0))
        first[r][2 * capacity :, :] = jnp.zeros((16, first[r].shape[1]), BF16)
        first[r][2 * capacity :, :capacity] = both.astype(BF16)


def diagonal(capacity):
    return lax.broadcasted_iota(jnp.int32, (capacity, 128), 0) == lax.broadcasted_iota(
        jnp.int32, (capacity, 128), 1
    )


def gate_column(piece, g, capacity):
    row = piece[2 * capacity :, :128].astype(F32)[g : g + 1, :]
    return jnp.sum(jnp.where(diagonal(capacity), row, 0.0), axis=1, keepdims=True)


def rest_kernel(block, capacity, chunks, take, own_ref, other_ref, matches_ref, *outs):
    if take:
        outs[-1][...] = outs[0][...]
        outs = outs[:-1]
    chip, _, _ = coordinates()
    tokens = own_ref.shape[0]
    for i, k in enumerate(chunks):
        columns = pl.ds(pl.multiple_of((chip ^ (3 - k)) * block, block), block)
        to = slice(i * block, (i + 1) * block)
        for g in range(2):
            rows = (own_ref if g == 0 else other_ref)[:tokens, columns]
            for r in range(4):
                outs[r - 4][g * capacity : (g + 1) * capacity, to] = dot(
                    matches_ref[g, r], rows, ((1,), (0,))
                ).astype(BF16)


def split_rows(pieces, at_columns, capacity, all_ref, own_ref, cross_ref):
    slots = 4 * capacity
    for r, piece in enumerate(pieces):
        at = slice(r * capacity, (r + 1) * capacity)
        mine = piece[:capacity, at_columns]
        cross = piece[capacity : 2 * capacity, at_columns]
        own_ref[at, :] = mine
        cross_ref[at, :] = cross
        all_ref[at, :] = mine
        all_ref[slots + r * capacity : slots + (r + 1) * capacity, :] = cross


def first_kernel(
    capacity, p0, p1, p2, p3, hidden_ref, other_ref, low_ref, high_ref, scaled_ref, own_ref, cross_ref, all_ref
):
    _, _, peer = coordinates()
    pieces = (p0, p1, p2, p3)
    for r, piece in enumerate(pieces):
        source = pl.ds(pl.multiple_of((peer ^ r) * capacity, 32), capacity)
        for g, hidden in enumerate((hidden_ref, other_ref)):
            at = slice((4 * g + r) * capacity, (4 * g + r + 1) * capacity)
            gate = gate_column(piece, g, capacity)
            scaled_ref[at, :] = (gate * hidden[source, :].astype(F32)).astype(BF16)
    split_rows(pieces, slice(None), capacity, all_ref, own_ref, cross_ref)
    part = dot(all_ref[...], scaled_ref[...], ((0,), (0,))).astype(BF16)
    half = low_ref.shape[0]
    low_ref[...] = part[:half, :]
    high_ref[...] = part[half:, :]


def second_kernel(capacity, p0, p1, p2, p3, scaled_ref, low_ref, high_ref, sum_ref, own_ref, cross_ref, all_ref):
    block = own_ref.shape[1]
    split_rows((p0, p1, p2, p3), slice(0, block), capacity, all_ref, own_ref, cross_ref)
    part = dot(all_ref[...], scaled_ref[...], ((0,), (0,)))
    half = low_ref.shape[0]
    sum_ref[:half, :] = (part[:half, :] + low_ref[...].astype(F32)).astype(BF16)
    sum_ref[half:, :] = (part[half:, :] + high_ref[...].astype(F32)).astype(BF16)


def last_kernel(capacity, p0, p1, p2, p3, scaled_ref, _, part2_ref, part3_ref, own2, cross2, own3, cross3, all_ref):
    for i, (part, own, cross) in enumerate(((part2_ref, own2, cross2), (part3_ref, own3, cross3))):
        block = own.shape[1]
        at = slice(i * block, (i + 1) * block)
        split_rows((p0, p1, p2, p3), at, capacity, all_ref.at[i], own, cross)
        part[...] = dot(all_ref[i], scaled_ref[...], ((0,), (0,))).astype(part.dtype)


def update_kernel(capacity, *refs):
    rows, (p0, p1, p2, p3, hidden_ref, weight_ref, out_ref, *pairs) = refs[:8], refs[8:]
    chip, core, peer = coordinates()
    block = rows[0].shape[1]
    update = None
    for k in range(4):
        for i, side in enumerate((core, 1 - core)):
            start = pl.multiple_of((2 * (chip ^ (3 - k)) + side) * block, block)
            term = dot(rows[2 * k + i][...], weight_ref[:, pl.ds(start, block)], ((1,), (1,)))
            update = term if update is None else update + term
    for r, piece in enumerate((p0, p1, p2, p3)):
        source = pl.ds(pl.multiple_of((peer ^ r) * capacity, 32), capacity)
        here = update[r * capacity : (r + 1) * capacity, :]
        out_ref[source, :] = (gate_column(piece, 0, capacity) * here).astype(BF16)
        pair = jnp.sum(hidden_ref[source, :].astype(F32) * here, axis=1, keepdims=True)
        line = jnp.sum(jnp.where(diagonal(capacity), pair, 0.0), axis=0, keepdims=True)
        pairs[r][...] = jnp.broadcast_to(line, (8, 128))


def gate_kernel(ids_ref, matches_ref, b0, b1, b2, b3, out_ref):
    _, _, peer = coordinates()
    ids = ids_ref[...]
    total = jnp.zeros(ids.shape, F32)
    for r, back in enumerate((b0, b1, b2, b3)):
        match = matches_ref[0, r].astype(F32)
        column = jnp.sum(
            jnp.where(diagonal(match.shape[0]), back[0:1, :], 0.0), axis=1, keepdims=True
        )
        at_token = jnp.sum(jnp.where(match > 0.0, column, 0.0), axis=0, keepdims=True)
        total = jnp.where(ids == (peer ^ r) * EXP_DEV, at_token, total)
    out_ref[...] = total


HBM = pl.BlockSpec(memory_space=pltpu.HBM)
ANY = pl.BlockSpec(memory_space=pl.ANY)
VMEM = pl.BlockSpec(memory_space=pltpu.VMEM)


def call(kernel, outs, specs=None, scratch=(), vmem=40 * 2**20):
    def run(*args):
        return pl.pallas_call(
            kernel,
            out_shape=outs,
            in_specs=specs or [VMEM] * len(args),
            out_specs=jax.tree.map(lambda _: VMEM, outs),
            scratch_shapes=list(scratch),
            compiler_params=pltpu.CompilerParams(vmem_limit_bytes=vmem),
            cost_estimate=pl.CostEstimate(flops=0, bytes_accessed=0, transcendentals=0),
        )(*args)

    return run


def arr(shape, dtype):
    return jax.ShapeDtypeStruct(shape, dtype)


def over(axis, size, mask):
    pairs = [(i, i ^ mask) for i in range(size)]
    return lambda x: lax.ppermute(x, axis, pairs)


def per_device(grad_out, expert_ids, gate_weights, saved_hidden, down_weight):
    groups, peers = lax.axis_size("dp"), lax.axis_size("expert")
    tokens, features = grad_out.shape
    hidden, weight = saved_hidden[0], down_weight[0]
    slots, units = hidden.shape
    capacity = slots // peers
    block = features // groups
    half = features // 2
    core_swap, near, far = (over("dp", groups, m) for m in (1, 2, 4))
    to_peer = [lambda x: x] + [over("expert", peers, r) for r in range(1, peers)]
    ids_t, gates_t = expert_ids.T, gate_weights.T

    hit = ids_t == EXP_DEV * jnp.arange(peers, dtype=jnp.int32)[:, None, None]
    marks = jnp.max(jnp.where(hit, gates_t, -jnp.ones((), BF16)), axis=1).astype(F32)
    send, own, marks = call(
        functools.partial(swap_kernel, block),
        [arr((tokens + 16, half), BF16), arr((tokens, half), BF16), arr((16, tokens), BF16)],
    )(marks, grad_out)
    other = core_swap(send)
    *first, matches = call(
        functools.partial(gather_kernel, block, capacity),
        [arr((2 * capacity + 16, block), BF16)] * peers
        + [arr((2, peers, capacity, tokens), BF16)],
        scratch=[pltpu.VMEM((4, 16, tokens), F32)],
    )(own, marks, other)
    first = [to_peer[r](first[r]) for r in range(peers)]
    other_hidden = core_swap(hidden)

    def later(chunks, *after, take=False):
        pieces = call(
            functools.partial(rest_kernel, block, capacity, chunks, take),
            [arr((2 * capacity, len(chunks) * block), BF16)] * peers
            + ([arr(after[0].shape, BF16)] if take else []),
            specs=[VMEM] * 3 + [VMEM if take else ANY] + [ANY] * (len(after) - 1),
        )(own, other, matches, *after)
        sent = [to_peer[r](pieces[r]) for r in range(peers)]
        return (sent, pieces[peers]) if take else sent

    one, hidden = later((1,), hidden, take=True)
    stack = (2 * slots, block)
    mine = arr((slots, block), BF16)
    low, high, scaled, own0, cross0 = call(
        functools.partial(first_kernel, capacity),
        [arr((block // 2, units), BF16)] * 2 + [arr((2 * slots, units), BF16), mine, mine],
        scratch=[pltpu.VMEM(stack, BF16)],
    )(*first, hidden, other_hidden)
    rest = later((2, 3), low)
    low, high = near(low), near(high)
    summed, own1, cross1 = call(
        functools.partial(second_kernel, capacity),
        [arr((block, units), BF16), mine, mine],
        scratch=[pltpu.VMEM(stack, BF16)],
    )(*one, scaled, low, high)
    come1 = far(summed)
    part2, part3, own2, cross2, own3, cross3 = call(
        functools.partial(last_kernel, capacity),
        [arr((block, units), BF16), arr((block, units), F32), mine, mine, mine, mine],
        specs=[VMEM] * 5 + [ANY],
        scratch=[pltpu.VMEM((2,) + stack, BF16)],
    )(*rest, scaled, summed)
    come2 = near(part2)
    rows = []
    for own_k, cross_k in ((own0, cross0), (own1, cross1), (own2, cross2), (own3, cross3)):
        rows += [own_k, core_swap(cross_k)]
    grad_hidden, *pairs = call(
        functools.partial(update_kernel, capacity),
        [arr((slots, units), BF16)] + [arr((8, 128), F32)] * peers,
    )(*rows, *first, hidden, weight)
    back = [to_peer[r](pairs[r]) for r in range(peers)]
    gate_grad = call(gate_kernel, arr((TOP, tokens), F32))(ids_t, matches, *back).T
    weight_grad = part3 + come2.astype(F32) + come1.astype(F32)
    return grad_hidden[None], gate_grad, weight_grad[None]


def solution(mesh):
    placed = (
        P(("dp", "expert"), None),
        P(("dp", "expert"), None),
        P(("dp", "expert"), None),
        P("expert", "dp", None),
        P("expert", None, None),
    )
    small = mesh.shape["dp"] == 8 and mesh.shape["expert"] == 4
    return jax.shard_map(
        per_device if small else per_device_general,
        mesh=mesh,
        in_specs=placed,
        out_specs=(P("expert", "dp", None), P(("dp", "expert"), None), P("expert", "dp", None)),
        check_vma=False,
    )
```

```python
import functools

import jax
import jax.numpy as jnp
from jax import lax
from jax.experimental import pallas as pl
from jax.experimental.pallas import tpu as pltpu
from jax.sharding import PartitionSpec as P

TOP = 8
EXP_DEV = 4
F32 = jnp.float32
BF16 = jnp.bfloat16
GATE_LANES = 128


def per_device_general(grad_out, expert_ids, gate_weights, saved_hidden, down_weight):
    peer_count = lax.axis_size("expert")
    tok_rows = grad_out.shape[0]
    capacity = saved_hidden.shape[1] // peer_count
    slot_total = peer_count * capacity
    flat_ids = expert_ids.reshape(-1)
    flight = flat_ids % EXP_DEV == 0
    target = flat_ids // EXP_DEV
    onehot = (
        (target[:, None] == jnp.arange(peer_count, dtype=jnp.int32)[None, :]) & flight[:, None]
    ).astype(jnp.int32)
    slot_rank = jnp.cumsum(onehot, axis=0) - 1
    slot_index = jnp.sum(slot_rank * onehot, axis=1)
    slot_place = jnp.where(flight, target * capacity + slot_index, slot_total)
    slot_match = slot_place[None, :] == jnp.arange(slot_total, dtype=jnp.int32)[:, None]
    gates_flat = gate_weights.astype(F32).reshape(-1)
    send_gates = jnp.sum(jnp.where(slot_match, gates_flat[None, :], 0.0), axis=1).astype(BF16)
    token_match = jnp.any(slot_match.reshape(slot_total, tok_rows, TOP), axis=2).astype(BF16)
    send_rows = jnp.dot(token_match, grad_out, preferred_element_type=F32).astype(BF16)
    exchange = functools.partial(
        lax.all_to_all, axis_name="expert", split_axis=0, concat_axis=0, tiled=True
    )
    rows_in = exchange(send_rows.reshape(peer_count, capacity, -1))
    gates_in = exchange(send_gates.reshape(peer_count, capacity))
    slot_rows = rows_in.reshape(slot_total, -1)
    slot_gates = gates_in.reshape(slot_total).astype(F32)
    hidden = saved_hidden[0]
    weight = down_weight[0]
    update = lax.dot_general(
        slot_rows, weight, (((1,), (1,)), ((), ())), preferred_element_type=F32
    )
    grad_hidden = (slot_gates[:, None] * update).astype(BF16)
    pair_grad = jnp.sum(hidden.astype(F32) * update, axis=1)
    returned = exchange(pair_grad.reshape(peer_count, capacity))
    gate_flat = jnp.sum(jnp.where(slot_match, returned.reshape(slot_total)[:, None], 0.0), axis=0)
    gate_grad = gate_flat.reshape(tok_rows, TOP)
    scaled = (slot_gates[:, None] * hidden.astype(F32)).astype(BF16)
    grad_term = lax.dot_general(
        slot_rows, scaled, (((0,), (0,)), ((), ())), preferred_element_type=F32
    )
    weight_shard = lax.psum_scatter(grad_term, "dp", scatter_dimension=0, tiled=True)
    return (grad_hidden[None], gate_grad, weight_shard[None])


def coordinates():
    group = lax.axis_index("dp")
    return group // 2, group % 2, lax.axis_index("expert")


def dot(a, b, dims):
    return lax.dot_general(a, b, (dims, ((), ())), preferred_element_type=F32)


def swap_kernel(block, marks_in, grad_ref, send_ref, own_ref, marks_ref):
    _, core, _ = coordinates()
    tokens = grad_ref.shape[0]
    for i in range(own_ref.shape[1] // block):
        at = slice(i * block, (i + 1) * block)
        for side, ref in ((1 - core, send_ref), (core, own_ref)):
            start = pl.multiple_of((2 * i + side) * block, block)
            ref[:tokens, at] = grad_ref[:, pl.ds(start, block)]
    marks = jnp.concatenate([marks_in[...], jnp.full((12, tokens), -1.0, F32)], axis=0)
    marks_ref[...] = marks.astype(BF16)
    send_ref[tokens:, :] = jnp.zeros((16, send_ref.shape[1]), BF16)
    send_ref[tokens:, :tokens] = marks.astype(BF16)


def gather_kernel(block, capacity, own_ref, marks_ref, other_ref, *outs):
    first, (matches_ref, scratch) = outs[:-2], outs[-2:]
    chip, _, peer = coordinates()
    tokens = own_ref.shape[0]
    before = (
        lax.broadcasted_iota(jnp.int32, (tokens, tokens), 0)
        < lax.broadcasted_iota(jnp.int32, (tokens, tokens), 1)
    ).astype(F32).astype(BF16)
    slot = lax.broadcasted_iota(jnp.int32, (capacity, tokens), 0).astype(F32)
    columns = pl.ds(pl.multiple_of((chip ^ 3) * block, block), block)
    gate_rows = [[], [], [], []]
    for g in range(2):
        marks = (marks_ref[...] if g == 0 else other_ref[tokens:, :tokens]).astype(F32)
        live = jnp.where(marks >= 0.0, 1.0, 0.0)
        rank = dot(live.astype(BF16), before, ((1,), (0,)))
        scratch[2 * g] = marks
        scratch[2 * g + 1] = jnp.where(marks >= 0.0, rank, -1.0)
        rows = (own_ref if g == 0 else other_ref)[:tokens, columns]
        for r in range(4):
            e = peer ^ r
            gate = scratch[2 * g, pl.ds(e, 1), :]
            place = scratch[2 * g + 1, pl.ds(e, 1), :]
            match = jnp.where(slot == place, 1.0, 0.0).astype(BF16)
            matches_ref[g, r] = match
            gate_rows[r].append(
                dot(jnp.broadcast_to(gate, (16, tokens)).astype(BF16), match, ((1,), (1,)))
            )
            first[r][g * capacity : (g + 1) * capacity, :] = dot(
                match, rows, ((1,), (0,))
            ).astype(BF16)
    row = lax.broadcasted_iota(jnp.int32, (16, capacity), 0)
    for r in range(4):
        both = jnp.where(row == 0, gate_rows[r][0], jnp.where(row == 1, gate_rows[r][1], 0.0))
        first[r][2 * capacity :, :] = jnp.zeros((16, first[r].shape[1]), BF16)
        first[r][2 * capacity :, :capacity] = both.astype(BF16)


def diagonal(capacity):
    return lax.broadcasted_iota(jnp.int32, (capacity, 128), 0) == lax.broadcasted_iota(
        jnp.int32, (capacity, 128), 1
    )


def gate_column(piece, g, capacity):
    row = piece[2 * capacity :, :128].astype(F32)[g : g + 1, :]
    return jnp.sum(jnp.where(diagonal(capacity), row, 0.0), axis=1, keepdims=True)


def rest_kernel(block, capacity, chunks, take, own_ref, other_ref, matches_ref, *outs):
    if take:
        outs[-1][...] = outs[0][...]
        outs = outs[:-1]
    chip, _, _ = coordinates()
    tokens = own_ref.shape[0]
    for i, k in enumerate(chunks):
        columns = pl.ds(pl.multiple_of((chip ^ (3 - k)) * block, block), block)
        to = slice(i * block, (i + 1) * block)
        for g in range(2):
            rows = (own_ref if g == 0 else other_ref)[:tokens, columns]
            for r in range(4):
                outs[r - 4][g * capacity : (g + 1) * capacity, to] = dot(
                    matches_ref[g, r], rows, ((1,), (0,))
                ).astype(BF16)


def split_rows(pieces, at_columns, capacity, all_ref, own_ref, cross_ref):
    slots = 4 * capacity
    for r, piece in enumerate(pieces):
        at = slice(r * capacity, (r + 1) * capacity)
        mine = piece[:capacity, at_columns]
        cross = piece[capacity : 2 * capacity, at_columns]
        own_ref[at, :] = mine
        cross_ref[at, :] = cross
        all_ref[at, :] = mine
        all_ref[slots + r * capacity : slots + (r + 1) * capacity, :] = cross


def first_kernel(
    capacity, p0, p1, p2, p3, hidden_ref, other_ref, low_ref, high_ref, scaled_ref, own_ref, cross_ref, all_ref
):
    _, _, peer = coordinates()
    pieces = (p0, p1, p2, p3)
    for r, piece in enumerate(pieces):
        source = pl.ds(pl.multiple_of((peer ^ r) * capacity, 32), capacity)
        for g, hidden in enumerate((hidden_ref, other_ref)):
            at = slice((4 * g + r) * capacity, (4 * g + r + 1) * capacity)
            gate = gate_column(piece, g, capacity)
            scaled_ref[at, :] = (gate * hidden[source, :].astype(F32)).astype(BF16)
    split_rows(pieces, slice(None), capacity, all_ref, own_ref, cross_ref)
    part = dot(all_ref[...], scaled_ref[...], ((0,), (0,))).astype(BF16)
    half = low_ref.shape[0]
    low_ref[...] = part[:half, :]
    high_ref[...] = part[half:, :]


def second_kernel(capacity, p0, p1, p2, p3, scaled_ref, low_ref, high_ref, sum_ref, own_ref, cross_ref, all_ref):
    block = own_ref.shape[1]
    split_rows((p0, p1, p2, p3), slice(0, block), capacity, all_ref, own_ref, cross_ref)
    part = dot(all_ref[...], scaled_ref[...], ((0,), (0,)))
    half = low_ref.shape[0]
    sum_ref[:half, :] = (part[:half, :] + low_ref[...].astype(F32)).astype(BF16)
    sum_ref[half:, :] = (part[half:, :] + high_ref[...].astype(F32)).astype(BF16)


def last_kernel(capacity, p0, p1, p2, p3, scaled_ref, _, part2_ref, part3_ref, own2, cross2, own3, cross3, all_ref):
    for i, (part, own, cross) in enumerate(((part2_ref, own2, cross2), (part3_ref, own3, cross3))):
        block = own.shape[1]
        at = slice(i * block, (i + 1) * block)
        split_rows((p0, p1, p2, p3), at, capacity, all_ref.at[i], own, cross)
        part[...] = dot(all_ref[i], scaled_ref[...], ((0,), (0,))).astype(part.dtype)


def update_kernel(capacity, *refs):
    rows, (p0, p1, p2, p3, hidden_ref, weight_ref, out_ref, *pairs) = refs[:8], refs[8:]
    chip, core, peer = coordinates()
    block = rows[0].shape[1]
    update = None
    for k in range(4):
        for i, side in enumerate((core, 1 - core)):
            start = pl.multiple_of((2 * (chip ^ (3 - k)) + side) * block, block)
            term = dot(rows[2 * k + i][...], weight_ref[:, pl.ds(start, block)], ((1,), (1,)))
            update = term if update is None else update + term
    for r, piece in enumerate((p0, p1, p2, p3)):
        source = pl.ds(pl.multiple_of((peer ^ r) * capacity, 32), capacity)
        here = update[r * capacity : (r + 1) * capacity, :]
        out_ref[source, :] = (gate_column(piece, 0, capacity) * here).astype(BF16)
        pair = jnp.sum(hidden_ref[source, :].astype(F32) * here, axis=1, keepdims=True)
        line = jnp.sum(jnp.where(diagonal(capacity), pair, 0.0), axis=0, keepdims=True)
        pairs[r][...] = jnp.broadcast_to(line, (8, 128))


def gate_kernel(ids_ref, matches_ref, b0, b1, b2, b3, part_ref, far_ref, out_ref, sum_ref):
    _, _, peer = coordinates()
    ids = ids_ref[...]
    total = jnp.zeros(ids.shape, F32)
    for r, back in enumerate((b0, b1, b2, b3)):
        match = matches_ref[0, r].astype(F32)
        column = jnp.sum(
            jnp.where(diagonal(match.shape[0]), back[0:1, :], 0.0), axis=1, keepdims=True
        )
        at_token = jnp.sum(jnp.where(match > 0.0, column, 0.0), axis=0, keepdims=True)
        total = jnp.where(ids == (peer ^ r) * EXP_DEV, at_token, total)
    out_ref[...] = total
    sum_ref[...] = part_ref[...] + far_ref[...].astype(F32)


HBM = pl.BlockSpec(memory_space=pltpu.HBM)
ANY = pl.BlockSpec(memory_space=pl.ANY)
VMEM = pl.BlockSpec(memory_space=pltpu.VMEM)


def call(kernel, outs, specs=None, scratch=(), cost=0, vmem=40 * 2**20):
    def run(*args):
        return pl.pallas_call(
            kernel,
            out_shape=outs,
            in_specs=specs or [VMEM] * len(args),
            out_specs=jax.tree.map(lambda _: VMEM, outs),
            scratch_shapes=list(scratch),
            compiler_params=pltpu.CompilerParams(vmem_limit_bytes=vmem),
            cost_estimate=pl.CostEstimate(flops=0, bytes_accessed=cost, transcendentals=0),
        )(*args)

    return run


def arr(shape, dtype):
    return jax.ShapeDtypeStruct(shape, dtype)


def over(axis, size, mask):
    pairs = [(i, i ^ mask) for i in range(size)]
    return lambda x: lax.ppermute(x, axis, pairs)


def per_device(grad_out, expert_ids, gate_weights, saved_hidden, down_weight):
    groups, peers = lax.axis_size("dp"), lax.axis_size("expert")
    tokens, features = grad_out.shape
    hidden, weight = saved_hidden[0], down_weight[0]
    slots, units = hidden.shape
    capacity = slots // peers
    block = features // groups
    half = features // 2
    core_swap, near, far = (over("dp", groups, m) for m in (1, 2, 4))
    to_peer = [lambda x: x] + [over("expert", peers, r) for r in range(1, peers)]
    ids_t, gates_t = expert_ids.T, gate_weights.T

    hit = ids_t == EXP_DEV * jnp.arange(peers, dtype=jnp.int32)[:, None, None]
    marks = jnp.max(jnp.where(hit, gates_t, -jnp.ones((), BF16)), axis=1).astype(F32)
    send, own, marks = call(
        functools.partial(swap_kernel, block),
        [arr((tokens + 16, half), BF16), arr((tokens, half), BF16), arr((16, tokens), BF16)],
    )(marks, grad_out)
    other = core_swap(send)
    *first, matches = call(
        functools.partial(gather_kernel, block, capacity),
        [arr((2 * capacity + 16, block), BF16)] * peers
        + [arr((2, peers, capacity, tokens), BF16)],
        scratch=[pltpu.VMEM((4, 16, tokens), F32)],
    )(own, marks, other)
    first = [to_peer[r](first[r]) for r in range(peers)]
    other_hidden = core_swap(hidden)

    def later(chunks, *after, take=False):
        pieces = call(
            functools.partial(rest_kernel, block, capacity, chunks, take),
            [arr((2 * capacity, len(chunks) * block), BF16)] * peers
            + ([arr(after[0].shape, BF16)] if take else []),
            specs=[VMEM] * 3 + [VMEM if take else ANY] + [ANY] * (len(after) - 1),
        )(own, other, matches, *after)
        sent = [to_peer[r](pieces[r]) for r in range(peers)]
        return (sent, pieces[peers]) if take else sent

    one, hidden = later((1,), hidden, take=True)
    stack = (2 * slots, block)
    mine = arr((slots, block), BF16)
    low, high, scaled, own0, cross0 = call(
        functools.partial(first_kernel, capacity),
        [arr((block // 2, units), BF16)] * 2 + [arr((2 * slots, units), BF16), mine, mine],
        scratch=[pltpu.VMEM(stack, BF16)],
    )(*first, hidden, other_hidden)
    rest = later((2, 3), low)
    low, high = near(low), near(high)
    summed, own1, cross1 = call(
        functools.partial(second_kernel, capacity),
        [arr((block, units), BF16), mine, mine],
        scratch=[pltpu.VMEM(stack, BF16)],
    )(*one, scaled, low, high)
    come1 = far(summed)
    part2, part3, own2, cross2, own3, cross3 = call(
        functools.partial(last_kernel, capacity),
        [arr((block, units), BF16), arr((block, units), F32), mine, mine, mine, mine],
        specs=[VMEM] * 5 + [ANY],
        scratch=[pltpu.VMEM((2,) + stack, BF16)],
    )(*rest, scaled, summed)
    come2 = near(part2)
    rows = []
    for own_k, cross_k in ((own0, cross0), (own1, cross1), (own2, cross2), (own3, cross3)):
        rows += [own_k, core_swap(cross_k)]
    grad_hidden, *pairs = call(
        functools.partial(update_kernel, capacity),
        [arr((slots, units), BF16)] + [arr((8, 128), F32)] * peers,
    )(*rows, *first, hidden, weight)
    back = [to_peer[r](pairs[r]) for r in range(peers)]
    gate_grad, most = call(
        gate_kernel, [arr((TOP, tokens), F32), arr((block, units), F32)], cost=4 * block * units
    )(ids_t, matches, *back, part3, come1)
    weight_grad = most + come2.astype(F32)
    return grad_hidden[None], gate_grad.T, weight_grad[None]


def solution(mesh):
    placed = (
        P(("dp", "expert"), None),
        P(("dp", "expert"), None),
        P(("dp", "expert"), None),
        P("expert", "dp", None),
        P("expert", None, None),
    )
    small = mesh.shape["dp"] == 8 and mesh.shape["expert"] == 4
    return jax.shard_map(
        per_device if small else per_device_general,
        mesh=mesh,
        in_specs=placed,
        out_specs=(P("expert", "dp", None), P(("dp", "expert"), None), P("expert", "dp", None)),
        check_vma=False,
    )
```

```python
import functools

import jax
import jax.numpy as jnp
from jax import lax
from jax.experimental import pallas as pl
from jax.experimental.pallas import tpu as pltpu
from jax.sharding import PartitionSpec as P

TOP = 8
EXP_DEV = 4
F32 = jnp.float32
BF16 = jnp.bfloat16
GATE_LANES = 128


def per_device_general(grad_out, expert_ids, gate_weights, saved_hidden, down_weight):
    peer_count = lax.axis_size("expert")
    tok_rows = grad_out.shape[0]
    capacity = saved_hidden.shape[1] // peer_count
    slot_total = peer_count * capacity
    flat_ids = expert_ids.reshape(-1)
    flight = flat_ids % EXP_DEV == 0
    target = flat_ids // EXP_DEV
    onehot = (
        (target[:, None] == jnp.arange(peer_count, dtype=jnp.int32)[None, :]) & flight[:, None]
    ).astype(jnp.int32)
    slot_rank = jnp.cumsum(onehot, axis=0) - 1
    slot_index = jnp.sum(slot_rank * onehot, axis=1)
    slot_place = jnp.where(flight, target * capacity + slot_index, slot_total)
    slot_match = slot_place[None, :] == jnp.arange(slot_total, dtype=jnp.int32)[:, None]
    gates_flat = gate_weights.astype(F32).reshape(-1)
    send_gates = jnp.sum(jnp.where(slot_match, gates_flat[None, :], 0.0), axis=1).astype(BF16)
    token_match = jnp.any(slot_match.reshape(slot_total, tok_rows, TOP), axis=2).astype(BF16)
    send_rows = jnp.dot(token_match, grad_out, preferred_element_type=F32).astype(BF16)
    exchange = functools.partial(
        lax.all_to_all, axis_name="expert", split_axis=0, concat_axis=0, tiled=True
    )
    rows_in = exchange(send_rows.reshape(peer_count, capacity, -1))
    gates_in = exchange(send_gates.reshape(peer_count, capacity))
    slot_rows = rows_in.reshape(slot_total, -1)
    slot_gates = gates_in.reshape(slot_total).astype(F32)
    hidden = saved_hidden[0]
    weight = down_weight[0]
    update = lax.dot_general(
        slot_rows, weight, (((1,), (1,)), ((), ())), preferred_element_type=F32
    )
    grad_hidden = (slot_gates[:, None] * update).astype(BF16)
    pair_grad = jnp.sum(hidden.astype(F32) * update, axis=1)
    returned = exchange(pair_grad.reshape(peer_count, capacity))
    gate_flat = jnp.sum(jnp.where(slot_match, returned.reshape(slot_total)[:, None], 0.0), axis=0)
    gate_grad = gate_flat.reshape(tok_rows, TOP)
    scaled = (slot_gates[:, None] * hidden.astype(F32)).astype(BF16)
    grad_term = lax.dot_general(
        slot_rows, scaled, (((0,), (0,)), ((), ())), preferred_element_type=F32
    )
    weight_shard = lax.psum_scatter(grad_term, "dp", scatter_dimension=0, tiled=True)
    return (grad_hidden[None], gate_grad, weight_shard[None])


def coordinates():
    group = lax.axis_index("dp")
    return group // 2, group % 2, lax.axis_index("expert")


def dot(a, b, dims):
    return lax.dot_general(a, b, (dims, ((), ())), preferred_element_type=F32)


def copy_kernel(from_ref, to_ref):
    to_ref[...] = from_ref[...]


def gather_kernel(block, capacity, own_ref, marks_ref, other_ref, other_marks_ref, *outs):
    first, (matches_ref, scratch) = outs[:-2], outs[-2:]
    chip, core, peer = coordinates()
    tokens = own_ref.shape[0]
    before = (
        lax.broadcasted_iota(jnp.int32, (tokens, tokens), 0)
        < lax.broadcasted_iota(jnp.int32, (tokens, tokens), 1)
    ).astype(F32).astype(BF16)
    slot = lax.broadcasted_iota(jnp.int32, (capacity, tokens), 0).astype(F32)
    columns = pl.ds(pl.multiple_of((2 * (chip ^ 3) + core) * block, block), block)
    gate_rows = [[], [], [], []]
    for g in range(2):
        marks = (marks_ref if g == 0 else other_marks_ref)[...].astype(F32)
        live = jnp.where(marks >= 0.0, 1.0, 0.0)
        rank = dot(live.astype(BF16), before, ((1,), (0,)))
        scratch[2 * g] = marks
        scratch[2 * g + 1] = jnp.where(marks >= 0.0, rank, -1.0)
        rows = (own_ref if g == 0 else other_ref)[:, columns]
        for r in range(4):
            e = peer ^ r
            gate = scratch[2 * g, pl.ds(e, 1), :]
            place = scratch[2 * g + 1, pl.ds(e, 1), :]
            match = jnp.where(slot == place, 1.0, 0.0).astype(BF16)
            matches_ref[g, r] = match
            gate_rows[r].append(
                dot(jnp.broadcast_to(gate, (16, tokens)).astype(BF16), match, ((1,), (1,)))
            )
            first[r][g * capacity : (g + 1) * capacity, :] = dot(
                match, rows, ((1,), (0,))
            ).astype(BF16)
    row = lax.broadcasted_iota(jnp.int32, (16, capacity), 0)
    for r in range(4):
        both = jnp.where(row == 0, gate_rows[r][0], jnp.where(row == 1, gate_rows[r][1], 0.0))
        first[r][2 * capacity :, :] = jnp.zeros((16, first[r].shape[1]), BF16)
        first[r][2 * capacity :, :capacity] = both.astype(BF16)


def diagonal(capacity):
    return lax.broadcasted_iota(jnp.int32, (capacity, 128), 0) == lax.broadcasted_iota(
        jnp.int32, (capacity, 128), 1
    )


def gate_column(piece, g, capacity):
    row = piece[2 * capacity :, :128].astype(F32)[g : g + 1, :]
    return jnp.sum(jnp.where(diagonal(capacity), row, 0.0), axis=1, keepdims=True)


def rest_kernel(block, capacity, chunks, take, own_ref, other_ref, matches_ref, *outs):
    if take:
        outs[-1][...] = outs[0][...]
        outs = outs[:-1]
    chip, core, _ = coordinates()
    for i, k in enumerate(chunks):
        columns = pl.ds(pl.multiple_of((2 * (chip ^ (3 - k)) + core) * block, block), block)
        to = slice(i * block, (i + 1) * block)
        for g in range(2):
            rows = (own_ref if g == 0 else other_ref)[:, columns]
            for r in range(4):
                outs[r - 4][g * capacity : (g + 1) * capacity, to] = dot(
                    matches_ref[g, r], rows, ((1,), (0,))
                ).astype(BF16)


def split_rows(pieces, at_columns, capacity, all_ref, own_ref, cross_ref):
    slots = 4 * capacity
    for r, piece in enumerate(pieces):
        at = slice(r * capacity, (r + 1) * capacity)
        mine = piece[:capacity, at_columns]
        cross = piece[capacity : 2 * capacity, at_columns]
        own_ref[at, :] = mine
        cross_ref[at, :] = cross
        all_ref[at, :] = mine
        all_ref[slots + r * capacity : slots + (r + 1) * capacity, :] = cross


def first_kernel(
    capacity, p0, p1, p2, p3, hidden_ref, other_ref, low_ref, high_ref, scaled_ref, own_ref, cross_ref, all_ref
):
    _, _, peer = coordinates()
    pieces = (p0, p1, p2, p3)
    for r, piece in enumerate(pieces):
        source = pl.ds(pl.multiple_of((peer ^ r) * capacity, 32), capacity)
        for g, hidden in enumerate((hidden_ref, other_ref)):
            at = slice((4 * g + r) * capacity, (4 * g + r + 1) * capacity)
            gate = gate_column(piece, g, capacity)
            scaled_ref[at, :] = (gate * hidden[source, :].astype(F32)).astype(BF16)
    split_rows(pieces, slice(None), capacity, all_ref, own_ref, cross_ref)
    part = dot(all_ref[...], scaled_ref[...], ((0,), (0,))).astype(BF16)
    half = low_ref.shape[0]
    low_ref[...] = part[:half, :]
    high_ref[...] = part[half:, :]


def second_kernel(capacity, p0, p1, p2, p3, scaled_ref, low_ref, high_ref, sum_ref, own_ref, cross_ref, all_ref):
    block = own_ref.shape[1]
    split_rows((p0, p1, p2, p3), slice(0, block), capacity, all_ref, own_ref, cross_ref)
    part = dot(all_ref[...], scaled_ref[...], ((0,), (0,)))
    half = low_ref.shape[0]
    sum_ref[:half, :] = (part[:half, :] + low_ref[...].astype(F32)).astype(BF16)
    sum_ref[half:, :] = (part[half:, :] + high_ref[...].astype(F32)).astype(BF16)


def last_kernel(capacity, p0, p1, p2, p3, scaled_ref, _, part2_ref, part3_ref, own2, cross2, own3, cross3, all_ref):
    for i, (part, own, cross) in enumerate(((part2_ref, own2, cross2), (part3_ref, own3, cross3))):
        block = own.shape[1]
        at = slice(i * block, (i + 1) * block)
        split_rows((p0, p1, p2, p3), at, capacity, all_ref.at[i], own, cross)
        part[...] = dot(all_ref[i], scaled_ref[...], ((0,), (0,))).astype(part.dtype)


def update_kernel(capacity, *refs):
    rows, (p0, p1, p2, p3, hidden_ref, weight_ref, out_ref, *pairs) = refs[:8], refs[8:]
    chip, core, peer = coordinates()
    block = rows[0].shape[1]
    update = None
    for k in range(4):
        for i, side in enumerate((core, 1 - core)):
            start = pl.multiple_of((2 * (chip ^ (3 - k)) + side) * block, block)
            term = dot(rows[2 * k + i][...], weight_ref[:, pl.ds(start, block)], ((1,), (1,)))
            update = term if update is None else update + term
    for r, piece in enumerate((p0, p1, p2, p3)):
        source = pl.ds(pl.multiple_of((peer ^ r) * capacity, 32), capacity)
        here = update[r * capacity : (r + 1) * capacity, :]
        out_ref[source, :] = (gate_column(piece, 0, capacity) * here).astype(BF16)
        pair = jnp.sum(hidden_ref[source, :].astype(F32) * here, axis=1, keepdims=True)
        line = jnp.sum(jnp.where(diagonal(capacity), pair, 0.0), axis=0, keepdims=True)
        pairs[r][...] = jnp.broadcast_to(line, (8, 128))


def gate_kernel(ids_ref, matches_ref, b0, b1, b2, b3, part_ref, far_ref, out_ref, sum_ref):
    _, _, peer = coordinates()
    ids = ids_ref[...]
    total = jnp.zeros(ids.shape, F32)
    for r, back in enumerate((b0, b1, b2, b3)):
        match = matches_ref[0, r].astype(F32)
        column = jnp.sum(
            jnp.where(diagonal(match.shape[0]), back[0:1, :], 0.0), axis=1, keepdims=True
        )
        at_token = jnp.sum(jnp.where(match > 0.0, column, 0.0), axis=0, keepdims=True)
        total = jnp.where(ids == (peer ^ r) * EXP_DEV, at_token, total)
    out_ref[...] = total
    sum_ref[...] = part_ref[...] + far_ref[...].astype(F32)


HBM = pl.BlockSpec(memory_space=pltpu.HBM)
ANY = pl.BlockSpec(memory_space=pl.ANY)
VMEM = pl.BlockSpec(memory_space=pltpu.VMEM)


def call(kernel, outs, specs=None, scratch=(), cost=0, vmem=40 * 2**20):
    def run(*args):
        return pl.pallas_call(
            kernel,
            out_shape=outs,
            in_specs=specs or [VMEM] * len(args),
            out_specs=jax.tree.map(lambda _: VMEM, outs),
            scratch_shapes=list(scratch),
            compiler_params=pltpu.CompilerParams(vmem_limit_bytes=vmem),
            cost_estimate=pl.CostEstimate(flops=0, bytes_accessed=cost, transcendentals=0),
        )(*args)

    return run


def arr(shape, dtype):
    return jax.ShapeDtypeStruct(shape, dtype)


def over(axis, size, mask):
    pairs = [(i, i ^ mask) for i in range(size)]
    return lambda x: lax.ppermute(x, axis, pairs)


def per_device(grad_out, expert_ids, gate_weights, saved_hidden, down_weight):
    groups, peers = lax.axis_size("dp"), lax.axis_size("expert")
    tokens, features = grad_out.shape
    hidden, weight = saved_hidden[0], down_weight[0]
    slots, units = hidden.shape
    capacity = slots // peers
    block = features // groups
    half = features // 2
    core_swap, near, far = (over("dp", groups, m) for m in (1, 2, 4))
    to_peer = [lambda x: x] + [over("expert", peers, r) for r in range(1, peers)]
    ids_t, gates_t = expert_ids.T, gate_weights.T

    hit = ids_t == EXP_DEV * jnp.arange(16, dtype=jnp.int32)[:, None, None]
    marks = jnp.max(jnp.where(hit, gates_t, -jnp.ones((), BF16)), axis=1)
    other, other_marks = core_swap(grad_out), core_swap(marks)
    own = call(copy_kernel, arr(grad_out.shape, BF16))(grad_out)
    *first, matches = call(
        functools.partial(gather_kernel, block, capacity),
        [arr((2 * capacity + 16, block), BF16)] * peers
        + [arr((2, peers, capacity, tokens), BF16)],
        scratch=[pltpu.VMEM((4, 16, tokens), F32)],
    )(own, marks, other, other_marks)
    first = [to_peer[r](first[r]) for r in range(peers)]
    other_hidden = core_swap(hidden)

    def later(chunks, *after, take=False):
        pieces = call(
            functools.partial(rest_kernel, block, capacity, chunks, take),
            [arr((2 * capacity, len(chunks) * block), BF16)] * peers
            + ([arr(after[0].shape, BF16)] if take else []),
            specs=[VMEM] * 3 + [VMEM if take else ANY] + [ANY] * (len(after) - 1),
        )(own, other, matches, *after)
        sent = [to_peer[r](pieces[r]) for r in range(peers)]
        return (sent, pieces[peers]) if take else sent

    one, hidden = later((1,), hidden, take=True)
    stack = (2 * slots, block)
    mine = arr((slots, block), BF16)
    low, high, scaled, own0, cross0 = call(
        functools.partial(first_kernel, capacity),
        [arr((block // 2, units), BF16)] * 2 + [arr((2 * slots, units), BF16), mine, mine],
        scratch=[pltpu.VMEM(stack, BF16)],
    )(*first, hidden, other_hidden)
    rest = later((2, 3), low)
    low, high = near(low), near(high)
    summed, own1, cross1 = call(
        functools.partial(second_kernel, capacity),
        [arr((block, units), BF16), mine, mine],
        scratch=[pltpu.VMEM(stack, BF16)],
    )(*one, scaled, low, high)
    come1 = far(summed)
    part2, part3, own2, cross2, own3, cross3 = call(
        functools.partial(last_kernel, capacity),
        [arr((block, units), BF16), arr((block, units), F32), mine, mine, mine, mine],
        specs=[VMEM] * 5 + [ANY],
        scratch=[pltpu.VMEM((2,) + stack, BF16)],
    )(*rest, scaled, summed)
    come2 = near(part2)
    rows = []
    for own_k, cross_k in ((own0, cross0), (own1, cross1), (own2, cross2), (own3, cross3)):
        rows += [own_k, core_swap(cross_k)]
    grad_hidden, *pairs = call(
        functools.partial(update_kernel, capacity),
        [arr((slots, units), BF16)] + [arr((8, 128), F32)] * peers,
    )(*rows, *first, hidden, weight)
    back = [to_peer[r](pairs[r]) for r in range(peers)]
    gate_grad, most = call(
        gate_kernel, [arr((TOP, tokens), F32), arr((block, units), F32)], cost=4 * block * units
    )(ids_t, matches, *back, part3, come1)
    weight_grad = most + come2.astype(F32)
    return grad_hidden[None], gate_grad.T, weight_grad[None]


def solution(mesh):
    placed = (
        P(("dp", "expert"), None),
        P(("dp", "expert"), None),
        P(("dp", "expert"), None),
        P("expert", "dp", None),
        P("expert", None, None),
    )
    small = mesh.shape["dp"] == 8 and mesh.shape["expert"] == 4
    return jax.shard_map(
        per_device if small else per_device_general,
        mesh=mesh,
        in_specs=placed,
        out_specs=(P("expert", "dp", None), P(("dp", "expert"), None), P("expert", "dp", None)),
        check_vma=False,
    )
```

```python
import functools

import jax
import jax.numpy as jnp
from jax import lax
from jax.experimental import pallas as pl
from jax.experimental.pallas import tpu as pltpu
from jax.sharding import PartitionSpec as P

TOP = 8
EXP_DEV = 4
F32 = jnp.float32
BF16 = jnp.bfloat16
GATE_LANES = 128


def per_device_general(grad_out, expert_ids, gate_weights, saved_hidden, down_weight):
    peer_count = lax.axis_size("expert")
    tok_rows = grad_out.shape[0]
    capacity = saved_hidden.shape[1] // peer_count
    slot_total = peer_count * capacity
    flat_ids = expert_ids.reshape(-1)
    flight = flat_ids % EXP_DEV == 0
    target = flat_ids // EXP_DEV
    onehot = (
        (target[:, None] == jnp.arange(peer_count, dtype=jnp.int32)[None, :]) & flight[:, None]
    ).astype(jnp.int32)
    slot_rank = jnp.cumsum(onehot, axis=0) - 1
    slot_index = jnp.sum(slot_rank * onehot, axis=1)
    slot_place = jnp.where(flight, target * capacity + slot_index, slot_total)
    slot_match = slot_place[None, :] == jnp.arange(slot_total, dtype=jnp.int32)[:, None]
    gates_flat = gate_weights.astype(F32).reshape(-1)
    send_gates = jnp.sum(jnp.where(slot_match, gates_flat[None, :], 0.0), axis=1).astype(BF16)
    token_match = jnp.any(slot_match.reshape(slot_total, tok_rows, TOP), axis=2).astype(BF16)
    send_rows = jnp.dot(token_match, grad_out, preferred_element_type=F32).astype(BF16)
    exchange = functools.partial(
        lax.all_to_all, axis_name="expert", split_axis=0, concat_axis=0, tiled=True
    )
    rows_in = exchange(send_rows.reshape(peer_count, capacity, -1))
    gates_in = exchange(send_gates.reshape(peer_count, capacity))
    slot_rows = rows_in.reshape(slot_total, -1)
    slot_gates = gates_in.reshape(slot_total).astype(F32)
    hidden = saved_hidden[0]
    weight = down_weight[0]
    update = lax.dot_general(
        slot_rows, weight, (((1,), (1,)), ((), ())), preferred_element_type=F32
    )
    grad_hidden = (slot_gates[:, None] * update).astype(BF16)
    pair_grad = jnp.sum(hidden.astype(F32) * update, axis=1)
    returned = exchange(pair_grad.reshape(peer_count, capacity))
    gate_flat = jnp.sum(jnp.where(slot_match, returned.reshape(slot_total)[:, None], 0.0), axis=0)
    gate_grad = gate_flat.reshape(tok_rows, TOP)
    scaled = (slot_gates[:, None] * hidden.astype(F32)).astype(BF16)
    grad_term = lax.dot_general(
        slot_rows, scaled, (((0,), (0,)), ((), ())), preferred_element_type=F32
    )
    weight_shard = lax.psum_scatter(grad_term, "dp", scatter_dimension=0, tiled=True)
    return (grad_hidden[None], gate_grad, weight_shard[None])


def coordinates():
    group = lax.axis_index("dp")
    return group // 2, group % 2, lax.axis_index("expert")


def dot(a, b, dims):
    return lax.dot_general(a, b, (dims, ((), ())), preferred_element_type=F32)


def copy_kernel(from_ref, to_ref):
    to_ref[...] = from_ref[...]


def gather_kernel(block, capacity, own_ref, marks_ref, other_ref, other_marks_ref, *outs):
    first, (matches_ref, scratch) = outs[:-2], outs[-2:]
    chip, core, peer = coordinates()
    tokens = own_ref.shape[0]
    before = (
        lax.broadcasted_iota(jnp.int32, (tokens, tokens), 0)
        < lax.broadcasted_iota(jnp.int32, (tokens, tokens), 1)
    ).astype(F32).astype(BF16)
    slot = lax.broadcasted_iota(jnp.int32, (capacity, tokens), 0).astype(F32)
    columns = pl.ds(pl.multiple_of((2 * (chip ^ 3) + core) * block, block), block)
    gate_rows = [[], [], [], []]
    for g in range(2):
        marks = (marks_ref if g == 0 else other_marks_ref)[...].astype(F32)
        live = jnp.where(marks >= 0.0, 1.0, 0.0)
        rank = dot(live.astype(BF16), before, ((1,), (0,)))
        scratch[2 * g] = marks
        scratch[2 * g + 1] = jnp.where(marks >= 0.0, rank, -1.0)
        rows = (own_ref if g == 0 else other_ref)[:, columns]
        for r in range(4):
            e = peer ^ r
            gate = scratch[2 * g, pl.ds(e, 1), :]
            place = scratch[2 * g + 1, pl.ds(e, 1), :]
            match = jnp.where(slot == place, 1.0, 0.0).astype(BF16)
            matches_ref[g, r] = match
            gate_rows[r].append(
                dot(jnp.broadcast_to(gate, (16, tokens)).astype(BF16), match, ((1,), (1,)))
            )
            first[r][g * capacity : (g + 1) * capacity, :] = dot(
                match, rows, ((1,), (0,))
            ).astype(BF16)
    row = lax.broadcasted_iota(jnp.int32, (16, capacity), 0)
    for r in range(4):
        both = jnp.where(row == 0, gate_rows[r][0], jnp.where(row == 1, gate_rows[r][1], 0.0))
        first[r][2 * capacity :, :] = jnp.zeros((16, first[r].shape[1]), BF16)
        first[r][2 * capacity :, :capacity] = both.astype(BF16)


def diagonal(capacity):
    return lax.broadcasted_iota(jnp.int32, (capacity, 128), 0) == lax.broadcasted_iota(
        jnp.int32, (capacity, 128), 1
    )


def gate_column(piece, g, capacity):
    row = piece[2 * capacity :, :128].astype(F32)[g : g + 1, :]
    return jnp.sum(jnp.where(diagonal(capacity), row, 0.0), axis=1, keepdims=True)


def rest_kernel(block, capacity, chunks, take, own_ref, other_ref, matches_ref, *outs):
    if take:
        outs[-1][...] = outs[0][...]
        outs = outs[:-1]
    chip, core, _ = coordinates()
    for i, k in enumerate(chunks):
        columns = pl.ds(pl.multiple_of((2 * (chip ^ (3 - k)) + core) * block, block), block)
        to = slice(i * block, (i + 1) * block)
        for g in range(2):
            rows = (own_ref if g == 0 else other_ref)[:, columns]
            for r in range(4):
                outs[r - 4][g * capacity : (g + 1) * capacity, to] = dot(
                    matches_ref[g, r], rows, ((1,), (0,))
                ).astype(BF16)


def split_rows(pieces, at_columns, capacity, all_ref, own_ref, cross_ref):
    slots = 4 * capacity
    for r, piece in enumerate(pieces):
        at = slice(r * capacity, (r + 1) * capacity)
        mine = piece[:capacity, at_columns]
        cross = piece[capacity : 2 * capacity, at_columns]
        own_ref[at, :] = mine
        cross_ref[at, :] = cross
        all_ref[at, :] = mine
        all_ref[slots + r * capacity : slots + (r + 1) * capacity, :] = cross


def first_kernel(
    capacity, p0, p1, p2, p3, hidden_ref, other_ref, low_ref, high_ref, scaled_ref, own_ref, cross_ref, all_ref
):
    _, _, peer = coordinates()
    pieces = (p0, p1, p2, p3)
    for r, piece in enumerate(pieces):
        source = pl.ds(pl.multiple_of((peer ^ r) * capacity, 32), capacity)
        for g, hidden in enumerate((hidden_ref, other_ref)):
            at = slice((4 * g + r) * capacity, (4 * g + r + 1) * capacity)
            gate = gate_column(piece, g, capacity)
            scaled_ref[at, :] = (gate * hidden[source, :].astype(F32)).astype(BF16)
    split_rows(pieces, slice(None), capacity, all_ref, own_ref, cross_ref)
    part = dot(all_ref[...], scaled_ref[...], ((0,), (0,))).astype(BF16)
    half = low_ref.shape[0]
    low_ref[...] = part[:half, :]
    high_ref[...] = part[half:, :]


def second_kernel(capacity, p0, p1, p2, p3, scaled_ref, low_ref, high_ref, sum_ref, own_ref, cross_ref, all_ref):
    block = own_ref.shape[1]
    split_rows((p0, p1, p2, p3), slice(0, block), capacity, all_ref, own_ref, cross_ref)
    part = dot(all_ref[...], scaled_ref[...], ((0,), (0,)))
    half = low_ref.shape[0]
    sum_ref[:half, :] = (part[:half, :] + low_ref[...].astype(F32)).astype(BF16)
    sum_ref[half:, :] = (part[half:, :] + high_ref[...].astype(F32)).astype(BF16)


def part_kernel(capacity, column, p0, p1, p2, p3, scaled_ref, _, part_ref, own_ref, cross_ref, all_ref):
    at = slice(column, column + own_ref.shape[1])
    split_rows((p0, p1, p2, p3), at, capacity, all_ref, own_ref, cross_ref)
    part_ref[...] = dot(all_ref[...], scaled_ref[...], ((0,), (0,))).astype(part_ref.dtype)


def update_kernel(capacity, *refs):
    rows, (p0, p1, p2, p3, hidden_ref, weight_ref, out_ref, *pairs) = refs[:8], refs[8:]
    chip, core, peer = coordinates()
    block = rows[0].shape[1]
    update = None
    for k in range(4):
        for i, side in enumerate((core, 1 - core)):
            start = pl.multiple_of((2 * (chip ^ (3 - k)) + side) * block, block)
            term = dot(rows[2 * k + i][...], weight_ref[:, pl.ds(start, block)], ((1,), (1,)))
            update = term if update is None else update + term
    for r, piece in enumerate((p0, p1, p2, p3)):
        source = pl.ds(pl.multiple_of((peer ^ r) * capacity, 32), capacity)
        here = update[r * capacity : (r + 1) * capacity, :]
        out_ref[source, :] = (gate_column(piece, 0, capacity) * here).astype(BF16)
        pair = jnp.sum(hidden_ref[source, :].astype(F32) * here, axis=1, keepdims=True)
        line = jnp.sum(jnp.where(diagonal(capacity), pair, 0.0), axis=0, keepdims=True)
        pairs[r][...] = jnp.broadcast_to(line, (8, 128))


def gate_kernel(ids_ref, matches_ref, b0, b1, b2, b3, part_ref, far_ref, out_ref, sum_ref):
    _, _, peer = coordinates()
    ids = ids_ref[...]
    total = jnp.zeros(ids.shape, F32)
    for r, back in enumerate((b0, b1, b2, b3)):
        match = matches_ref[0, r].astype(F32)
        column = jnp.sum(
            jnp.where(diagonal(match.shape[0]), back[0:1, :], 0.0), axis=1, keepdims=True
        )
        at_token = jnp.sum(jnp.where(match > 0.0, column, 0.0), axis=0, keepdims=True)
        total = jnp.where(ids == (peer ^ r) * EXP_DEV, at_token, total)
    out_ref[...] = total
    sum_ref[...] = part_ref[...] + far_ref[...].astype(F32)


HBM = pl.BlockSpec(memory_space=pltpu.HBM)
ANY = pl.BlockSpec(memory_space=pl.ANY)
VMEM = pl.BlockSpec(memory_space=pltpu.VMEM)


def call(kernel, outs, specs=None, scratch=(), cost=0, vmem=40 * 2**20):
    def run(*args):
        return pl.pallas_call(
            kernel,
            out_shape=outs,
            in_specs=specs or [VMEM] * len(args),
            out_specs=jax.tree.map(lambda _: VMEM, outs),
            scratch_shapes=list(scratch),
            compiler_params=pltpu.CompilerParams(vmem_limit_bytes=vmem),
            cost_estimate=pl.CostEstimate(flops=0, bytes_accessed=cost, transcendentals=0),
        )(*args)

    return run


def arr(shape, dtype):
    return jax.ShapeDtypeStruct(shape, dtype)


def over(axis, size, mask):
    pairs = [(i, i ^ mask) for i in range(size)]
    return lambda x: lax.ppermute(x, axis, pairs)


def per_device(grad_out, expert_ids, gate_weights, saved_hidden, down_weight):
    groups, peers = lax.axis_size("dp"), lax.axis_size("expert")
    tokens, features = grad_out.shape
    hidden, weight = saved_hidden[0], down_weight[0]
    slots, units = hidden.shape
    capacity = slots // peers
    block = features // groups
    half = features // 2
    core_swap, near, far = (over("dp", groups, m) for m in (1, 2, 4))
    to_peer = [lambda x: x] + [over("expert", peers, r) for r in range(1, peers)]
    ids_t, gates_t = expert_ids.T, gate_weights.T

    hit = ids_t == EXP_DEV * jnp.arange(16, dtype=jnp.int32)[:, None, None]
    marks = jnp.max(jnp.where(hit, gates_t, -jnp.ones((), BF16)), axis=1)
    other, other_marks = core_swap(grad_out), core_swap(marks)
    own = call(copy_kernel, arr(grad_out.shape, BF16))(grad_out)
    *first, matches = call(
        functools.partial(gather_kernel, block, capacity),
        [arr((2 * capacity + 16, block), BF16)] * peers
        + [arr((2, peers, capacity, tokens), BF16)],
        scratch=[pltpu.VMEM((4, 16, tokens), F32)],
    )(own, marks, other, other_marks)
    first = [to_peer[r](first[r]) for r in range(peers)]
    other_hidden = core_swap(hidden)

    def later(chunks, *after, take=False):
        pieces = call(
            functools.partial(rest_kernel, block, capacity, chunks, take),
            [arr((2 * capacity, len(chunks) * block), BF16)] * peers
            + ([arr(after[0].shape, BF16)] if take else []),
            specs=[VMEM] * 3 + [VMEM if take else ANY] + [ANY] * (len(after) - 1),
        )(own, other, matches, *after)
        sent = [to_peer[r](pieces[r]) for r in range(peers)]
        return (sent, pieces[peers]) if take else sent

    one, hidden = later((1,), hidden, take=True)
    stack = (2 * slots, block)
    mine = arr((slots, block), BF16)
    low, high, scaled, own0, cross0 = call(
        functools.partial(first_kernel, capacity),
        [arr((block // 2, units), BF16)] * 2 + [arr((2 * slots, units), BF16), mine, mine],
        scratch=[pltpu.VMEM(stack, BF16)],
    )(*first, hidden, other_hidden)
    rest = later((2, 3), low)
    low, high = near(low), near(high)
    summed, own1, cross1 = call(
        functools.partial(second_kernel, capacity),
        [arr((block, units), BF16), mine, mine],
        scratch=[pltpu.VMEM(stack, BF16)],
    )(*one, scaled, low, high)
    come1 = far(summed)
    def product(column, dtype, after):
        return call(
            functools.partial(part_kernel, capacity, column),
            [arr((block, units), dtype), mine, mine],
            specs=[VMEM] * 5 + [ANY],
            scratch=[pltpu.VMEM(stack, BF16)],
        )(*rest, scaled, after)

    part2, own2, cross2 = product(0, BF16, summed)
    part3, own3, cross3 = product(block, F32, part2)
    come2 = near(part2)
    rows = []
    for own_k, cross_k in ((own0, cross0), (own1, cross1), (own2, cross2), (own3, cross3)):
        rows += [own_k, core_swap(cross_k)]
    grad_hidden, *pairs = call(
        functools.partial(update_kernel, capacity),
        [arr((slots, units), BF16)] + [arr((8, 128), F32)] * peers,
    )(*rows, *first, hidden, weight)
    back = [to_peer[r](pairs[r]) for r in range(peers)]
    gate_grad, most = call(
        gate_kernel, [arr((TOP, tokens), F32), arr((block, units), F32)], cost=4 * block * units
    )(ids_t, matches, *back, part3, come1)
    weight_grad = most + come2.astype(F32)
    return grad_hidden[None], gate_grad.T, weight_grad[None]


def solution(mesh):
    placed = (
        P(("dp", "expert"), None),
        P(("dp", "expert"), None),
        P(("dp", "expert"), None),
        P("expert", "dp", None),
        P("expert", None, None),
    )
    small = mesh.shape["dp"] == 8 and mesh.shape["expert"] == 4
    return jax.shard_map(
        per_device if small else per_device_general,
        mesh=mesh,
        in_specs=placed,
        out_specs=(P("expert", "dp", None), P(("dp", "expert"), None), P("expert", "dp", None)),
        check_vma=False,
    )
```

```python
import functools

import jax
import jax.numpy as jnp
from jax import lax
from jax.experimental import pallas as pl
from jax.experimental.pallas import tpu as pltpu
from jax.sharding import PartitionSpec as P

TOP = 8
EXP_DEV = 4
F32 = jnp.float32
BF16 = jnp.bfloat16
GATE_LANES = 128


def per_device_general(grad_out, expert_ids, gate_weights, saved_hidden, down_weight):
    peer_count = lax.axis_size("expert")
    tok_rows = grad_out.shape[0]
    capacity = saved_hidden.shape[1] // peer_count
    slot_total = peer_count * capacity
    flat_ids = expert_ids.reshape(-1)
    flight = flat_ids % EXP_DEV == 0
    target = flat_ids // EXP_DEV
    onehot = (
        (target[:, None] == jnp.arange(peer_count, dtype=jnp.int32)[None, :]) & flight[:, None]
    ).astype(jnp.int32)
    slot_rank = jnp.cumsum(onehot, axis=0) - 1
    slot_index = jnp.sum(slot_rank * onehot, axis=1)
    slot_place = jnp.where(flight, target * capacity + slot_index, slot_total)
    slot_match = slot_place[None, :] == jnp.arange(slot_total, dtype=jnp.int32)[:, None]
    gates_flat = gate_weights.astype(F32).reshape(-1)
    send_gates = jnp.sum(jnp.where(slot_match, gates_flat[None, :], 0.0), axis=1).astype(BF16)
    token_match = jnp.any(slot_match.reshape(slot_total, tok_rows, TOP), axis=2).astype(BF16)
    send_rows = jnp.dot(token_match, grad_out, preferred_element_type=F32).astype(BF16)
    exchange = functools.partial(
        lax.all_to_all, axis_name="expert", split_axis=0, concat_axis=0, tiled=True
    )
    rows_in = exchange(send_rows.reshape(peer_count, capacity, -1))
    gates_in = exchange(send_gates.reshape(peer_count, capacity))
    slot_rows = rows_in.reshape(slot_total, -1)
    slot_gates = gates_in.reshape(slot_total).astype(F32)
    hidden = saved_hidden[0]
    weight = down_weight[0]
    update = lax.dot_general(
        slot_rows, weight, (((1,), (1,)), ((), ())), preferred_element_type=F32
    )
    grad_hidden = (slot_gates[:, None] * update).astype(BF16)
    pair_grad = jnp.sum(hidden.astype(F32) * update, axis=1)
    returned = exchange(pair_grad.reshape(peer_count, capacity))
    gate_flat = jnp.sum(jnp.where(slot_match, returned.reshape(slot_total)[:, None], 0.0), axis=0)
    gate_grad = gate_flat.reshape(tok_rows, TOP)
    scaled = (slot_gates[:, None] * hidden.astype(F32)).astype(BF16)
    grad_term = lax.dot_general(
        slot_rows, scaled, (((0,), (0,)), ((), ())), preferred_element_type=F32
    )
    weight_shard = lax.psum_scatter(grad_term, "dp", scatter_dimension=0, tiled=True)
    return (grad_hidden[None], gate_grad, weight_shard[None])


def coordinates():
    group = lax.axis_index("dp")
    return group // 2, group % 2, lax.axis_index("expert")


def dot(a, b, dims):
    return lax.dot_general(a, b, (dims, ((), ())), preferred_element_type=F32)


def copy_kernel(from_ref, to_ref):
    to_ref[...] = from_ref[...]


def gather_kernel(block, capacity, own_ref, marks_ref, other_ref, other_marks_ref, *outs):
    first, (matches_ref, scratch) = outs[:-2], outs[-2:]
    chip, core, peer = coordinates()
    tokens = own_ref.shape[0]
    before = (
        lax.broadcasted_iota(jnp.int32, (tokens, tokens), 0)
        < lax.broadcasted_iota(jnp.int32, (tokens, tokens), 1)
    ).astype(F32).astype(BF16)
    slot = lax.broadcasted_iota(jnp.int32, (capacity, tokens), 0).astype(F32)
    columns = pl.ds(pl.multiple_of((2 * (chip ^ 3) + core) * block, block), block)
    gate_rows = [[], [], [], []]
    for g in range(2):
        marks = (marks_ref if g == 0 else other_marks_ref)[...].astype(F32)
        live = jnp.where(marks >= 0.0, 1.0, 0.0)
        rank = dot(live.astype(BF16), before, ((1,), (0,)))
        scratch[2 * g] = marks
        scratch[2 * g + 1] = jnp.where(marks >= 0.0, rank, -1.0)
        rows = (own_ref if g == 0 else other_ref)[:, columns]
        for r in range(4):
            e = peer ^ r
            gate = scratch[2 * g, pl.ds(e, 1), :]
            place = scratch[2 * g + 1, pl.ds(e, 1), :]
            match = jnp.where(slot == place, 1.0, 0.0).astype(BF16)
            matches_ref[g, r] = match
            gate_rows[r].append(
                dot(jnp.broadcast_to(gate, (16, tokens)).astype(BF16), match, ((1,), (1,)))
            )
            first[r][g * capacity : (g + 1) * capacity, :] = dot(
                match, rows, ((1,), (0,))
            ).astype(BF16)
    row = lax.broadcasted_iota(jnp.int32, (16, capacity), 0)
    for r in range(4):
        both = jnp.where(row == 0, gate_rows[r][0], jnp.where(row == 1, gate_rows[r][1], 0.0))
        first[r][2 * capacity :, :] = jnp.zeros((16, first[r].shape[1]), BF16)
        first[r][2 * capacity :, :capacity] = both.astype(BF16)


def diagonal(capacity):
    return lax.broadcasted_iota(jnp.int32, (capacity, 128), 0) == lax.broadcasted_iota(
        jnp.int32, (capacity, 128), 1
    )


def gate_column(piece, g, capacity):
    row = piece[2 * capacity :, :128].astype(F32)[g : g + 1, :]
    return jnp.sum(jnp.where(diagonal(capacity), row, 0.0), axis=1, keepdims=True)


def rest_kernel(block, capacity, chunks, take, own_ref, other_ref, matches_ref, *outs):
    if take:
        outs[-1][...] = outs[0][...]
        outs = outs[:-1]
    chip, core, _ = coordinates()
    for i, k in enumerate(chunks):
        columns = pl.ds(pl.multiple_of((2 * (chip ^ (3 - k)) + core) * block, block), block)
        to = slice(i * block, (i + 1) * block)
        for g in range(2):
            rows = (own_ref if g == 0 else other_ref)[:, columns]
            for r in range(4):
                outs[r - 4][g * capacity : (g + 1) * capacity, to] = dot(
                    matches_ref[g, r], rows, ((1,), (0,))
                ).astype(BF16)


def split_rows(pieces, at_columns, capacity, all_ref, own_ref, cross_ref):
    slots = 4 * capacity
    for r, piece in enumerate(pieces):
        at = slice(r * capacity, (r + 1) * capacity)
        mine = piece[:capacity, at_columns]
        cross = piece[capacity : 2 * capacity, at_columns]
        own_ref[at, :] = mine
        cross_ref[at, :] = cross
        all_ref[at, :] = mine
        all_ref[slots + r * capacity : slots + (r + 1) * capacity, :] = cross


def first_kernel(
    capacity, p0, p1, p2, p3, hidden_ref, other_ref, low_ref, high_ref, scaled_ref, own_ref, cross_ref, all_ref
):
    _, _, peer = coordinates()
    pieces = (p0, p1, p2, p3)
    for r, piece in enumerate(pieces):
        source = pl.ds(pl.multiple_of((peer ^ r) * capacity, 32), capacity)
        for g, hidden in enumerate((hidden_ref, other_ref)):
            at = slice((4 * g + r) * capacity, (4 * g + r + 1) * capacity)
            gate = gate_column(piece, g, capacity)
            scaled_ref[at, :] = (gate * hidden[source, :].astype(F32)).astype(BF16)
    split_rows(pieces, slice(None), capacity, all_ref, own_ref, cross_ref)
    part = dot(all_ref[...], scaled_ref[...], ((0,), (0,))).astype(BF16)
    half = low_ref.shape[0]
    low_ref[...] = part[:half, :]
    high_ref[...] = part[half:, :]


def second_kernel(capacity, p0, p1, p2, p3, scaled_ref, low_ref, high_ref, sum_ref, own_ref, cross_ref, all_ref):
    block = own_ref.shape[1]
    split_rows((p0, p1, p2, p3), slice(0, block), capacity, all_ref, own_ref, cross_ref)
    part = dot(all_ref[...], scaled_ref[...], ((0,), (0,)))
    half = low_ref.shape[0]
    sum_ref[:half, :] = (part[:half, :] + low_ref[...].astype(F32)).astype(BF16)
    sum_ref[half:, :] = (part[half:, :] + high_ref[...].astype(F32)).astype(BF16)


def part_kernel(capacity, column, p0, p1, p2, p3, scaled_ref, _, part_ref, own_ref, cross_ref, all_ref):
    at = slice(column, column + own_ref.shape[1])
    split_rows((p0, p1, p2, p3), at, capacity, all_ref, own_ref, cross_ref)
    part_ref[...] = dot(all_ref[...], scaled_ref[...], ((0,), (0,))).astype(part_ref.dtype)


def update_kernel(capacity, *refs):
    rows, (p0, p1, p2, p3, hidden_ref, weight_ref, out_ref, *pairs) = refs[:8], refs[8:]
    chip, core, peer = coordinates()
    block = rows[0].shape[1]
    update = None
    for k in range(4):
        for i, side in enumerate((core, 1 - core)):
            start = pl.multiple_of((2 * (chip ^ (3 - k)) + side) * block, block)
            term = dot(rows[2 * k + i][...], weight_ref[:, pl.ds(start, block)], ((1,), (1,)))
            update = term if update is None else update + term
    for r, piece in enumerate((p0, p1, p2, p3)):
        source = pl.ds(pl.multiple_of((peer ^ r) * capacity, 32), capacity)
        here = update[r * capacity : (r + 1) * capacity, :]
        out_ref[source, :] = (gate_column(piece, 0, capacity) * here).astype(BF16)
        pair = jnp.sum(hidden_ref[source, :].astype(F32) * here, axis=1, keepdims=True)
        line = jnp.sum(jnp.where(diagonal(capacity), pair, 0.0), axis=0, keepdims=True)
        pairs[r][...] = jnp.broadcast_to(line, (8, 128))


def gate_kernel(ids_ref, matches_ref, b0, b1, b2, b3, part_ref, far_ref, out_ref, sum_ref):
    _, _, peer = coordinates()
    ids = ids_ref[...]
    total = jnp.zeros(ids.shape, F32)
    for r, back in enumerate((b0, b1, b2, b3)):
        match = matches_ref[0, r].astype(F32)
        column = jnp.sum(
            jnp.where(diagonal(match.shape[0]), back[0:1, :], 0.0), axis=1, keepdims=True
        )
        at_token = jnp.sum(jnp.where(match > 0.0, column, 0.0), axis=0, keepdims=True)
        total = jnp.where(ids == (peer ^ r) * EXP_DEV, at_token, total)
    out_ref[...] = total
    sum_ref[...] = part_ref[...] + far_ref[...].astype(F32)


HBM = pl.BlockSpec(memory_space=pltpu.HBM)
ANY = pl.BlockSpec(memory_space=pl.ANY)
VMEM = pl.BlockSpec(memory_space=pltpu.VMEM)


def call(kernel, outs, specs=None, scratch=(), cost=0, vmem=40 * 2**20):
    def run(*args):
        return pl.pallas_call(
            kernel,
            out_shape=outs,
            in_specs=specs or [VMEM] * len(args),
            out_specs=jax.tree.map(lambda _: VMEM, outs),
            scratch_shapes=list(scratch),
            compiler_params=pltpu.CompilerParams(vmem_limit_bytes=vmem),
            cost_estimate=pl.CostEstimate(flops=0, bytes_accessed=cost, transcendentals=0),
        )(*args)

    return run


def arr(shape, dtype):
    return jax.ShapeDtypeStruct(shape, dtype)


def over(axis, size, mask):
    pairs = [(i, i ^ mask) for i in range(size)]
    return lambda x: lax.ppermute(x, axis, pairs)


def per_device(grad_out, expert_ids, gate_weights, saved_hidden, down_weight):
    groups, peers = lax.axis_size("dp"), lax.axis_size("expert")
    tokens, features = grad_out.shape
    hidden, weight = saved_hidden[0], down_weight[0]
    slots, units = hidden.shape
    capacity = slots // peers
    block = features // groups
    half = features // 2
    core_swap, near, far = (over("dp", groups, m) for m in (1, 2, 4))
    to_peer = [lambda x: x] + [over("expert", peers, r) for r in range(1, peers)]
    ids_t, gates_t = expert_ids.T, gate_weights.T

    hit = ids_t == EXP_DEV * jnp.arange(16, dtype=jnp.int32)[:, None, None]
    marks = jnp.max(jnp.where(hit, gates_t, -jnp.ones((), BF16)), axis=1)
    other, other_marks = core_swap(grad_out), core_swap(marks)
    own = call(copy_kernel, arr(grad_out.shape, BF16))(grad_out)
    *first, matches = call(
        functools.partial(gather_kernel, block, capacity),
        [arr((2 * capacity + 16, block), BF16)] * peers
        + [arr((2, peers, capacity, tokens), BF16)],
        scratch=[pltpu.VMEM((4, 16, tokens), F32)],
    )(own, marks, other, other_marks)
    first = [to_peer[r](first[r]) for r in range(peers)]
    other_hidden = core_swap(hidden)

    def later(chunks, *after, take=False):
        pieces = call(
            functools.partial(rest_kernel, block, capacity, chunks, take),
            [arr((2 * capacity, len(chunks) * block), BF16)] * peers
            + ([arr(after[0].shape, BF16)] if take else []),
            specs=[VMEM] * 3 + [VMEM if take else ANY] + [ANY] * (len(after) - 1),
        )(own, other, matches, *after)
        sent = [to_peer[r](pieces[r]) for r in range(peers)]
        return (sent, pieces[peers]) if take else sent

    one = later((1,), matches)
    hidden = call(copy_kernel, arr((slots, units), BF16))(hidden)
    stack = (2 * slots, block)
    mine = arr((slots, block), BF16)
    low, high, scaled, own0, cross0 = call(
        functools.partial(first_kernel, capacity),
        [arr((block // 2, units), BF16)] * 2 + [arr((2 * slots, units), BF16), mine, mine],
        scratch=[pltpu.VMEM(stack, BF16)],
    )(*first, hidden, other_hidden)
    rest = later((2, 3), low)
    low, high = near(low), near(high)
    summed, own1, cross1 = call(
        functools.partial(second_kernel, capacity),
        [arr((block, units), BF16), mine, mine],
        scratch=[pltpu.VMEM(stack, BF16)],
    )(*one, scaled, low, high)
    come1 = far(summed)
    def product(column, dtype, after):
        return call(
            functools.partial(part_kernel, capacity, column),
            [arr((block, units), dtype), mine, mine],
            specs=[VMEM] * 5 + [ANY],
            scratch=[pltpu.VMEM(stack, BF16)],
        )(*rest, scaled, after)

    part2, own2, cross2 = product(0, BF16, summed)
    part3, own3, cross3 = product(block, F32, part2)
    come2 = near(part2)
    rows = []
    for own_k, cross_k in ((own0, cross0), (own1, cross1), (own2, cross2), (own3, cross3)):
        rows += [own_k, core_swap(cross_k)]
    grad_hidden, *pairs = call(
        functools.partial(update_kernel, capacity),
        [arr((slots, units), BF16)] + [arr((8, 128), F32)] * peers,
    )(*rows, *first, hidden, weight)
    back = [to_peer[r](pairs[r]) for r in range(peers)]
    gate_grad, most = call(
        gate_kernel, [arr((TOP, tokens), F32), arr((block, units), F32)], cost=4 * block * units
    )(ids_t, matches, *back, part3, come1)
    weight_grad = most + come2.astype(F32)
    return grad_hidden[None], gate_grad.T, weight_grad[None]


def solution(mesh):
    placed = (
        P(("dp", "expert"), None),
        P(("dp", "expert"), None),
        P(("dp", "expert"), None),
        P("expert", "dp", None),
        P("expert", None, None),
    )
    small = mesh.shape["dp"] == 8 and mesh.shape["expert"] == 4
    return jax.shard_map(
        per_device if small else per_device_general,
        mesh=mesh,
        in_specs=placed,
        out_specs=(P("expert", "dp", None), P(("dp", "expert"), None), P("expert", "dp", None)),
        check_vma=False,
    )
```

```python
import functools

import jax
import jax.numpy as jnp
from jax import lax
from jax.experimental import pallas as pl
from jax.experimental.pallas import tpu as pltpu
from jax.sharding import PartitionSpec as P

TOP = 8
EXP_DEV = 4
F32 = jnp.float32
BF16 = jnp.bfloat16
GATE_LANES = 128


def per_device_general(grad_out, expert_ids, gate_weights, saved_hidden, down_weight):
    peer_count = lax.axis_size("expert")
    tok_rows = grad_out.shape[0]
    capacity = saved_hidden.shape[1] // peer_count
    slot_total = peer_count * capacity
    flat_ids = expert_ids.reshape(-1)
    flight = flat_ids % EXP_DEV == 0
    target = flat_ids // EXP_DEV
    onehot = (
        (target[:, None] == jnp.arange(peer_count, dtype=jnp.int32)[None, :]) & flight[:, None]
    ).astype(jnp.int32)
    slot_rank = jnp.cumsum(onehot, axis=0) - 1
    slot_index = jnp.sum(slot_rank * onehot, axis=1)
    slot_place = jnp.where(flight, target * capacity + slot_index, slot_total)
    slot_match = slot_place[None, :] == jnp.arange(slot_total, dtype=jnp.int32)[:, None]
    gates_flat = gate_weights.astype(F32).reshape(-1)
    send_gates = jnp.sum(jnp.where(slot_match, gates_flat[None, :], 0.0), axis=1).astype(BF16)
    token_match = jnp.any(slot_match.reshape(slot_total, tok_rows, TOP), axis=2).astype(BF16)
    send_rows = jnp.dot(token_match, grad_out, preferred_element_type=F32).astype(BF16)
    exchange = functools.partial(
        lax.all_to_all, axis_name="expert", split_axis=0, concat_axis=0, tiled=True
    )
    rows_in = exchange(send_rows.reshape(peer_count, capacity, -1))
    gates_in = exchange(send_gates.reshape(peer_count, capacity))
    slot_rows = rows_in.reshape(slot_total, -1)
    slot_gates = gates_in.reshape(slot_total).astype(F32)
    hidden = saved_hidden[0]
    weight = down_weight[0]
    update = lax.dot_general(
        slot_rows, weight, (((1,), (1,)), ((), ())), preferred_element_type=F32
    )
    grad_hidden = (slot_gates[:, None] * update).astype(BF16)
    pair_grad = jnp.sum(hidden.astype(F32) * update, axis=1)
    returned = exchange(pair_grad.reshape(peer_count, capacity))
    gate_flat = jnp.sum(jnp.where(slot_match, returned.reshape(slot_total)[:, None], 0.0), axis=0)
    gate_grad = gate_flat.reshape(tok_rows, TOP)
    scaled = (slot_gates[:, None] * hidden.astype(F32)).astype(BF16)
    grad_term = lax.dot_general(
        slot_rows, scaled, (((0,), (0,)), ((), ())), preferred_element_type=F32
    )
    weight_shard = lax.psum_scatter(grad_term, "dp", scatter_dimension=0, tiled=True)
    return (grad_hidden[None], gate_grad, weight_shard[None])


def coordinates():
    group = lax.axis_index("dp")
    return group // 2, group % 2, lax.axis_index("expert")


def dot(a, b, dims):
    return lax.dot_general(a, b, (dims, ((), ())), preferred_element_type=F32)


def copy_kernel(from_ref, to_ref):
    to_ref[...] = from_ref[...]


def gather_kernel(block, capacity, own_ref, marks_ref, other_ref, other_marks_ref, *outs):
    first, (matches_ref, scratch) = outs[:-2], outs[-2:]
    chip, core, peer = coordinates()
    tokens = own_ref.shape[0]
    before = (
        lax.broadcasted_iota(jnp.int32, (tokens, tokens), 0)
        < lax.broadcasted_iota(jnp.int32, (tokens, tokens), 1)
    ).astype(F32).astype(BF16)
    slot = lax.broadcasted_iota(jnp.int32, (capacity, tokens), 0).astype(F32)
    columns = pl.ds(pl.multiple_of((2 * (chip ^ 3) + core) * block, block), block)
    gate_rows = [[], [], [], []]
    for g in range(2):
        marks = (marks_ref if g == 0 else other_marks_ref)[...].astype(F32)
        live = jnp.where(marks >= 0.0, 1.0, 0.0)
        rank = dot(live.astype(BF16), before, ((1,), (0,)))
        scratch[2 * g] = marks
        scratch[2 * g + 1] = jnp.where(marks >= 0.0, rank, -1.0)
        rows = (own_ref if g == 0 else other_ref)[:, columns]
        for r in range(4):
            e = peer ^ r
            gate = scratch[2 * g, pl.ds(e, 1), :]
            place = scratch[2 * g + 1, pl.ds(e, 1), :]
            match = jnp.where(slot == place, 1.0, 0.0).astype(BF16)
            matches_ref[g, r] = match
            gate_rows[r].append(
                dot(jnp.broadcast_to(gate, (16, tokens)).astype(BF16), match, ((1,), (1,)))
            )
            first[r][g * capacity : (g + 1) * capacity, :] = dot(
                match, rows, ((1,), (0,))
            ).astype(BF16)
    row = lax.broadcasted_iota(jnp.int32, (16, capacity), 0)
    for r in range(4):
        both = jnp.where(row == 0, gate_rows[r][0], jnp.where(row == 1, gate_rows[r][1], 0.0))
        first[r][2 * capacity :, :] = jnp.zeros((16, first[r].shape[1]), BF16)
        first[r][2 * capacity :, :capacity] = both.astype(BF16)


def diagonal(capacity):
    return lax.broadcasted_iota(jnp.int32, (capacity, 128), 0) == lax.broadcasted_iota(
        jnp.int32, (capacity, 128), 1
    )


def gate_column(piece, g, capacity):
    row = piece[2 * capacity :, :128].astype(F32)[g : g + 1, :]
    return jnp.sum(jnp.where(diagonal(capacity), row, 0.0), axis=1, keepdims=True)


def rest_kernel(block, capacity, chunks, take, own_ref, other_ref, matches_ref, *outs):
    if take:
        outs[-1][...] = outs[0][...]
        outs = outs[:-1]
    chip, core, _ = coordinates()
    for i, k in enumerate(chunks):
        columns = pl.ds(pl.multiple_of((2 * (chip ^ (3 - k)) + core) * block, block), block)
        to = slice(i * block, (i + 1) * block)
        for g in range(2):
            rows = (own_ref if g == 0 else other_ref)[:, columns]
            for r in range(4):
                outs[r - 4][g * capacity : (g + 1) * capacity, to] = dot(
                    matches_ref[g, r], rows, ((1,), (0,))
                ).astype(BF16)


def split_rows(pieces, at_columns, capacity, all_ref, own_ref, cross_ref):
    slots = 4 * capacity
    for r, piece in enumerate(pieces):
        at = slice(r * capacity, (r + 1) * capacity)
        mine = piece[:capacity, at_columns]
        cross = piece[capacity : 2 * capacity, at_columns]
        own_ref[at, :] = mine
        cross_ref[at, :] = cross
        all_ref[at, :] = mine
        all_ref[slots + r * capacity : slots + (r + 1) * capacity, :] = cross


def first_kernel(
    capacity, p0, p1, p2, p3, hidden_ref, other_ref, low_ref, high_ref, scaled_ref, own_ref, cross_ref, all_ref
):
    _, _, peer = coordinates()
    pieces = (p0, p1, p2, p3)
    for r, piece in enumerate(pieces):
        source = pl.ds(pl.multiple_of((peer ^ r) * capacity, 32), capacity)
        for g, hidden in enumerate((hidden_ref, other_ref)):
            at = slice((4 * g + r) * capacity, (4 * g + r + 1) * capacity)
            gate = gate_column(piece, g, capacity)
            scaled_ref[at, :] = (gate * hidden[source, :].astype(F32)).astype(BF16)
    split_rows(pieces, slice(None), capacity, all_ref, own_ref, cross_ref)
    part = dot(all_ref[...], scaled_ref[...], ((0,), (0,))).astype(BF16)
    half = low_ref.shape[0]
    low_ref[...] = part[:half, :]
    high_ref[...] = part[half:, :]


def second_kernel(capacity, p0, p1, p2, p3, scaled_ref, low_ref, high_ref, sum_ref, own_ref, cross_ref, all_ref):
    block = own_ref.shape[1]
    split_rows((p0, p1, p2, p3), slice(0, block), capacity, all_ref, own_ref, cross_ref)
    part = dot(all_ref[...], scaled_ref[...], ((0,), (0,)))
    half = low_ref.shape[0]
    sum_ref[:half, :] = (part[:half, :] + low_ref[...].astype(F32)).astype(BF16)
    sum_ref[half:, :] = (part[half:, :] + high_ref[...].astype(F32)).astype(BF16)


def part_kernel(capacity, column, p0, p1, p2, p3, scaled_ref, _, part_ref, own_ref, cross_ref, all_ref):
    at = slice(column, column + own_ref.shape[1])
    split_rows((p0, p1, p2, p3), at, capacity, all_ref, own_ref, cross_ref)
    part_ref[...] = dot(all_ref[...], scaled_ref[...], ((0,), (0,))).astype(part_ref.dtype)


def update_kernel(capacity, *refs):
    rows, (p0, p1, p2, p3, hidden_ref, weight_ref, out_ref, *pairs) = refs[:8], refs[8:]
    chip, core, peer = coordinates()
    block = rows[0].shape[1]
    update = None
    for k in range(4):
        for i, side in enumerate((core, 1 - core)):
            start = pl.multiple_of((2 * (chip ^ (3 - k)) + side) * block, block)
            term = dot(rows[2 * k + i][...], weight_ref[:, pl.ds(start, block)], ((1,), (1,)))
            update = term if update is None else update + term
    for r, piece in enumerate((p0, p1, p2, p3)):
        source = pl.ds(pl.multiple_of((peer ^ r) * capacity, 32), capacity)
        here = update[r * capacity : (r + 1) * capacity, :]
        out_ref[source, :] = (gate_column(piece, 0, capacity) * here).astype(BF16)
        pair = jnp.sum(hidden_ref[source, :].astype(F32) * here, axis=1, keepdims=True)
        line = jnp.sum(jnp.where(diagonal(capacity), pair, 0.0), axis=0, keepdims=True)
        pairs[r][...] = jnp.broadcast_to(line, (8, 128))


def gate_kernel(ids_ref, matches_ref, b0, b1, b2, b3, out_ref, done_ref):
    _, _, peer = coordinates()
    ids = ids_ref[...]
    total = jnp.zeros(ids.shape, F32)
    for r, back in enumerate((b0, b1, b2, b3)):
        match = matches_ref[0, r].astype(F32)
        column = jnp.sum(
            jnp.where(diagonal(match.shape[0]), back[0:1, :], 0.0), axis=1, keepdims=True
        )
        at_token = jnp.sum(jnp.where(match > 0.0, column, 0.0), axis=0, keepdims=True)
        total = jnp.where(ids == (peer ^ r) * EXP_DEV, at_token, total)
    out_ref[...] = total
    done_ref[...] = total


def far_kernel(part_ref, far_ref, _, sum_ref):
    sum_ref[...] = part_ref[...] + far_ref[...].astype(F32)


def total_kernel(part_ref, near_ref, out_hbm, total_ref, sems):
    size = total_ref.shape[0] // 4
    copies = []
    for i in range(4):
        at = pl.ds(i * size, size)
        total_ref[at, :] = part_ref[at, :] + near_ref[at, :].astype(F32)
        copy = pltpu.make_async_copy(total_ref.at[at, :], out_hbm.at[at, :], sems.at[i])
        copy.start()
        copies.append(copy)
    for copy in copies:
        copy.wait()


HBM = pl.BlockSpec(memory_space=pltpu.HBM)
ANY = pl.BlockSpec(memory_space=pl.ANY)
VMEM = pl.BlockSpec(memory_space=pltpu.VMEM)


def call(kernel, outs, specs=None, scratch=(), cost=0, outs_at=None, vmem=40 * 2**20):
    def run(*args):
        return pl.pallas_call(
            kernel,
            out_shape=outs,
            in_specs=specs or [VMEM] * len(args),
            out_specs=outs_at or jax.tree.map(lambda _: VMEM, outs),
            scratch_shapes=list(scratch),
            compiler_params=pltpu.CompilerParams(vmem_limit_bytes=vmem),
            cost_estimate=pl.CostEstimate(flops=0, bytes_accessed=cost, transcendentals=0),
        )(*args)

    return run


def arr(shape, dtype):
    return jax.ShapeDtypeStruct(shape, dtype)


def over(axis, size, mask):
    pairs = [(i, i ^ mask) for i in range(size)]
    return lambda x: lax.ppermute(x, axis, pairs)


def per_device(grad_out, expert_ids, gate_weights, saved_hidden, down_weight):
    groups, peers = lax.axis_size("dp"), lax.axis_size("expert")
    tokens, features = grad_out.shape
    hidden, weight = saved_hidden[0], down_weight[0]
    slots, units = hidden.shape
    capacity = slots // peers
    block = features // groups
    half = features // 2
    core_swap, near, far = (over("dp", groups, m) for m in (1, 2, 4))
    to_peer = [lambda x: x] + [over("expert", peers, r) for r in range(1, peers)]
    ids_t, gates_t = expert_ids.T, gate_weights.T

    hit = ids_t == EXP_DEV * jnp.arange(16, dtype=jnp.int32)[:, None, None]
    marks = jnp.max(jnp.where(hit, gates_t, -jnp.ones((), BF16)), axis=1)
    other, other_marks = core_swap(grad_out), core_swap(marks)
    own = call(copy_kernel, arr(grad_out.shape, BF16))(grad_out)
    *first, matches = call(
        functools.partial(gather_kernel, block, capacity),
        [arr((2 * capacity + 16, block), BF16)] * peers
        + [arr((2, peers, capacity, tokens), BF16)],
        scratch=[pltpu.VMEM((4, 16, tokens), F32)],
    )(own, marks, other, other_marks)
    first = [to_peer[r](first[r]) for r in range(peers)]
    other_hidden = core_swap(hidden)

    def later(chunks, *after, take=False):
        pieces = call(
            functools.partial(rest_kernel, block, capacity, chunks, take),
            [arr((2 * capacity, len(chunks) * block), BF16)] * peers
            + ([arr(after[0].shape, BF16)] if take else []),
            specs=[VMEM] * 3 + [VMEM if take else ANY] + [ANY] * (len(after) - 1),
        )(own, other, matches, *after)
        sent = [to_peer[r](pieces[r]) for r in range(peers)]
        return (sent, pieces[peers]) if take else sent

    one = later((1,), matches)
    hidden = call(copy_kernel, arr((slots, units), BF16))(hidden)
    stack = (2 * slots, block)
    mine = arr((slots, block), BF16)
    low, high, scaled, own0, cross0 = call(
        functools.partial(first_kernel, capacity),
        [arr((block // 2, units), BF16)] * 2 + [arr((2 * slots, units), BF16), mine, mine],
        scratch=[pltpu.VMEM(stack, BF16)],
    )(*first, hidden, other_hidden)
    rest = later((2, 3), low)
    low, high = near(low), near(high)
    summed, own1, cross1 = call(
        functools.partial(second_kernel, capacity),
        [arr((block, units), BF16), mine, mine],
        scratch=[pltpu.VMEM(stack, BF16)],
    )(*one, scaled, low, high)
    come1 = far(summed)
    def product(column, dtype, after):
        return call(
            functools.partial(part_kernel, capacity, column),
            [arr((block, units), dtype), mine, mine],
            specs=[VMEM] * 5 + [ANY],
            scratch=[pltpu.VMEM(stack, BF16)],
        )(*rest, scaled, after)

    part2, own2, cross2 = product(0, BF16, summed)
    part3, own3, cross3 = product(block, F32, part2)
    come2 = near(part2)
    rows = []
    for own_k, cross_k in ((own0, cross0), (own1, cross1), (own2, cross2), (own3, cross3)):
        rows += [own_k, core_swap(cross_k)]
    grad_hidden, *pairs = call(
        functools.partial(update_kernel, capacity),
        [arr((slots, units), BF16)] + [arr((8, 128), F32)] * peers,
    )(*rows, *first, hidden, weight)
    back = [to_peer[r](pairs[r]) for r in range(peers)]
    gate_grad, done = call(gate_kernel, [arr((TOP, tokens), F32)] * 2)(ids_t, matches, *back)
    most = call(
        far_kernel, arr((block, units), F32), specs=[VMEM] * 2 + [ANY], cost=4 * block * units
    )(part3, come1, done)
    weight_grad = call(
        total_kernel,
        arr((block, units), F32),
        outs_at=HBM,
        scratch=[pltpu.VMEM((block, units), F32), pltpu.SemaphoreType.DMA((4,))],
    )(most, come2)
    return grad_hidden[None], gate_grad.T, weight_grad[None]


def solution(mesh):
    placed = (
        P(("dp", "expert"), None),
        P(("dp", "expert"), None),
        P(("dp", "expert"), None),
        P("expert", "dp", None),
        P("expert", None, None),
    )
    small = mesh.shape["dp"] == 8 and mesh.shape["expert"] == 4
    return jax.shard_map(
        per_device if small else per_device_general,
        mesh=mesh,
        in_specs=placed,
        out_specs=(P("expert", "dp", None), P(("dp", "expert"), None), P("expert", "dp", None)),
        check_vma=False,
    )
```
